32 devices in a mesh: group: 2 (over x), batch: 8 (over z, y), mp: 2 (over core).
Axes of the slice: x: 2, y: 2, z: 4, core: 2. Of those that a mesh axis runs over, the one named last changes fastest.
Arguments:
- tokens: bfloat16 [256, 6144], P(('group', 'batch'), 'mp'), parts along dimension 0, may hold values from -6 to 6
- expert_ids: int32 [256, 2], P(('group', 'batch')), parts along dimension 0, may hold values from 0 to 3, all different within a row; in each aligned block of 128 rows (0 to 127, 128 to 255, ...) at most 96 rows name the same one
- router: bfloat16 [6144, 4], P('mp'), may hold values from -0.15625 to 0.15625
- w_gate: bfloat16 [4, 8192, 6144], P(None, 'batch', 'mp'), may hold values from -0.078125 to 0.078125
- w_up: bfloat16 [4, 8192, 6144], P(None, 'batch', 'mp'), may hold values from -0.078125 to 0.078125
- w_down: bfloat16 [4, 8192, 6144], P(None, 'batch', 'mp'), may hold values from -0.0625 to 0.0625
Outputs:
- expert_output: bfloat16 [256, 6144], P(('group', 'batch'), 'mp'), parts along dimension 0
The draws below stay inside these ranges and needn't reach their ends.
There are 2 independent parts, one for each index of `group`. The reference program is written for one: setup_inputs(seed, part) draws one part's arguments, and reference() takes and returns one part's arrays. A program takes and returns all parts, laid end to end along the dimension named above; an argument that names none is the same for every part. Nothing has to cross between parts.
Inputs may be any that keep to these rules, and one draw needn't show every extreme that they name: `expert_ids`: each token names two different experts; no expert is named by more than 96 tokens of a replica, a bound that some block reaches.
All inputs are finite; a program needn't handle non-finite values.
Results may differ from the reference program's by a relative error of at most 0.0051.
Values may be sent and summed in bfloat16 or wider, within the bound.
No kernel may reach another device: no remote copies, remote signals or barrier semaphores. Data moves between devices by JAX's collectives and lax.ppermute only.
A program may use at most 192 MiB of HBM per device.

```python
import math
import jax
import jax.numpy as jnp
import numpy as np

D = 6144
FF = 8192
EXPERTS = 4
TOP = 2
TOKENS = 128
CAP = 96


def shard_levels(own_key, dims, split, smallest, largest):
    loudness = 1.0
    for dim, blocks in split:
        steps = jax.random.uniform(jax.random.fold_in(jax.random.fold_in(own_key, 6), dim), (blocks,), jnp.float32, smallest / len(split), largest / len(split))
        loudness = loudness * jnp.repeat(jnp.exp(steps), dims[dim] // blocks).reshape((-1,) + (1,) * (len(dims) - 1 - dim))
    return loudness


def routed_block(rng, own, number, rows, amount, top, limit, skew):
    order = jax.random.permutation(rng, amount)
    heavy_load, usual = load_shares(amount, rows * top, limit, skew, True), load_shares(amount, rows * top, limit, skew, False)
    places = jnp.arange(amount)

    def named(tallies, offset_by):
        used = int((tallies > 0).sum())
        fixed = max(1, used // 4)
        shifted = fixed + (places - fixed + offset_by * (used - fixed)) % max(1, amount - fixed)
        return jnp.zeros((amount,), jnp.int32).at[order[jnp.where(places < fixed, places, shifted)]].set(jnp.asarray(tallies, jnp.int32))

    tallies = jnp.where(number % 4 == 0, named(heavy_load, number // 4), named(usual, number - number // 4 - 1))
    mixed = jax.random.permutation(jax.random.fold_in(own, 3), amount)
    giver, sink = mixed[0:amount // 2 * 2:2], mixed[1:amount // 2 * 2:2]
    room = jnp.minimum(tallies[giver] - 1, limit - tallies[sink]) // 2
    room = jnp.where((giver == order[0]) | (sink == order[0]) | (tallies[sink] == 0), 0, jnp.maximum(room, 0))
    shifted = jax.random.randint(jax.random.fold_in(own, 4), (amount // 2,), 0, 1 << 20) % (room + 1)
    tallies = tallies.at[giver].add(-shifted).at[sink].add(shifted)
    labels = jnp.searchsorted(jnp.cumsum(tallies), jnp.arange(rows * top), side="right").astype(jnp.int32)
    grid = labels.reshape(top, rows).T
    grid = grid[jax.random.permutation(jax.random.fold_in(own, 1), rows)]
    offset_by = jax.random.randint(jax.random.fold_in(own, 2), (rows, 1), 0, top)
    return jnp.take_along_axis(grid, (jnp.arange(top)[None, :] + offset_by) % top, axis=1)


def load_shares(number_of, total, most, skew, full):
    loads = [(1 << 20) // math.isqrt(rank ** skew) + 1 for rank in range(1, number_of + 1)]
    largest = most if full else min(most, max(-(-total // number_of), total * loads[0] // sum(loads)))
    least = 1 if total - largest >= number_of - 1 else 0
    given, rest = [largest] + [least] * (number_of - 1), total - largest - least * (number_of - 1)
    while rest > 0:
        movable = [i for i in range(1, number_of) if given[i] < largest] or [i for i in range(1, number_of) if given[i] < most]
        mass, left = sum([loads[i] for i in movable]), rest
        for i in movable:
            more = min(most - given[i], max(1, left * loads[i] // mass), rest)
            given[i] = given[i] + more
            rest = rest - more
    return np.array(given)


def normal_values(key, dims, spread, reach, pieces=(), held_as=jnp.bfloat16):
    entries = spread * jax.random.normal(key, dims, jnp.float32)
    if pieces:
        entries = entries * shard_levels(key, dims, pieces, -0.22, 0.18)
    return jnp.clip(entries, -reach, reach).astype(held_as)


def setup_inputs(seed: int = 0, part: int = 0) -> dict:
    keys = jax.random.split(jax.random.key(seed), 7)
    part_keys = jax.random.split(jax.random.fold_in(keys[6], part), 7)
    tokens = normal_values(part_keys[0], (TOKENS, D), 1.0, 6.0, ((0, 8), (1, 2)))
    expert_ids_keys = jax.random.split(jax.random.fold_in(part_keys[1], 1), TOKENS // TOKENS)
    expert_ids_turns = jax.random.permutation(jax.random.fold_in(part_keys[1], 3), TOKENS // TOKENS)
    expert_ids = jax.vmap(lambda own, number: routed_block(jax.random.fold_in(part_keys[1], 2), own, number, TOKENS, EXPERTS, TOP, CAP, 1))(expert_ids_keys, expert_ids_turns).reshape((TOKENS, TOP))
    router = normal_values(keys[2], (D, EXPERTS), (D // 4) ** -0.5, 0.15625, ((0, 2),))
    w_gate = normal_values(keys[3], (EXPERTS, FF, D), D ** -0.5, 0.078125, ((1, 8), (2, 2)))
    w_up = normal_values(keys[4], (EXPERTS, FF, D), D ** -0.5, 0.078125, ((1, 8), (2, 2)))
    w_down = normal_values(keys[5], (EXPERTS, FF, D), FF ** -0.5, 0.0625, ((1, 8), (2, 2)))
    return {"tokens": tokens, "expert_ids": expert_ids, "router": router, "w_gate": w_gate, "w_up": w_up, "w_down": w_down}


def reference(tokens, expert_ids, router, w_gate, w_up, w_down):
    logits = jnp.dot(tokens, router, preferred_element_type=jnp.float32)
    chosen = jnp.take_along_axis(logits, expert_ids, axis=1)
    weights = 1.0 / (1.0 + jnp.exp(chosen[:, ::-1] - chosen))
    result = jnp.zeros((tokens.shape[0], tokens.shape[1]), jnp.float32)
    for expert in range(EXPERTS):
        factor = jnp.sum(jnp.where(expert_ids == expert, weights, jnp.zeros_like(weights)), axis=1)
        gate_sum = jnp.dot(tokens, w_gate[expert].T, preferred_element_type=jnp.float32)
        up_sum = jnp.dot(tokens, w_up[expert].T, preferred_element_type=jnp.float32)
        hidden = (jax.nn.silu(gate_sum) * up_sum).astype(jnp.bfloat16)
        result = result + factor[:, None] * jnp.dot(hidden, w_down[expert], preferred_element_type=jnp.float32)
    return result.astype(jnp.bfloat16)
```

```python
import functools
import jax
import jax.numpy as jnp
from jax import lax
from jax.experimental import pallas as pl
from jax.experimental.pallas import tpu as pltpu
from jax.sharding import PartitionSpec as P

F32, BF16 = jnp.float32, jnp.bfloat16
IDS = 128
SWAP = [(0, 1), (1, 0)]
HBM_BLOCK = pl.BlockSpec(memory_space=pltpu.HBM)
VMEM_BLOCK = pl.BlockSpec(memory_space=pltpu.VMEM)


def xor_send(block, mask):
    return lax.ppermute(block, "batch", [(i, i ^ mask) for i in range(8)])


def in_vmem(array):
    return pltpu.with_memory_space_constraint(array, pltpu.VMEM)


def call(kernel, outs, args, flops, size, vmem, scratch=(), hbm=()):
    specs = [HBM_BLOCK if i in hbm else VMEM_BLOCK for i in range(len(args))]
    return pl.pallas_call(
        kernel,
        out_shape=outs,
        in_specs=specs,
        out_specs=[VMEM_BLOCK] * len(outs),
        scratch_shapes=list(scratch),
        compiler_params=pltpu.CompilerParams(vmem_limit_bytes=int(vmem * 2**20)),
        cost_estimate=pl.CostEstimate(flops=flops, bytes_accessed=size, transcendentals=0),
    )(*args)


def pack_kernel(tokens_ref, ids_ref, out_ref):
    rows, width = tokens_ref.shape
    out_ref[:, :width] = tokens_ref[...]
    ids = ids_ref[...].astype(F32)
    lane = lax.broadcasted_iota(jnp.int32, (rows, IDS), 1)
    out_ref[:, width:] = jnp.where(lane == 0, ids[:, 0:1], ids[:, 1:2]).astype(BF16)


def stream(w_ref, held_ref, sems, experts, part_ref, load):
    hidden, width = w_ref.shape[1:]
    slots, tile = held_ref.shape[:2]
    steps = [(e, f) for e in experts for f in range(0, hidden, tile)]

    def copy(step):
        e, f = steps[step]
        slot = step % slots
        return pltpu.make_async_copy(
            w_ref.at[e, pl.ds(f, tile)], held_ref.at[slot], sems.at[slot]
        )

    for step in range(min(slots, len(steps))):
        copy(step).start()
    x = load()
    for step in range(len(steps)):
        copy(step).wait()
        part_ref[step * tile : (step + 1) * tile] = jnp.dot(
            held_ref[step % slots], x, preferred_element_type=F32
        )
        if step + slots < len(steps):
            copy(step + slots).start()


def gate_kernel(*refs):
    blocks, (router_ref, w_ref, turned_ref, part_ref) = refs[:8], refs[8:12]
    rows_ref, held_ref, sems = refs[12:]
    experts, hidden, width = w_ref.shape

    def load():
        rows = blocks[0].shape[0]
        for j, block in enumerate(blocks):
            rows_ref[j * rows : (j + 1) * rows] = block[...].astype(F32)
        turned_ref[...] = rows_ref[...].T.astype(BF16)
        x = turned_ref[:width]
        part_ref[experts * hidden :] = jnp.dot(
            router_ref[...], x, preferred_element_type=F32
        )
        return x

    stream(w_ref, held_ref, sems, range(experts), part_ref, load)


def up_kernel(experts, turned_ref, w_ref, part_ref, held_ref, sems):
    width = w_ref.shape[2]
    stream(w_ref, held_ref, sems, experts, part_ref, lambda: turned_ref[:width])


def factors(turned_ref, gate_a, gate_b, width, base, experts):
    ids = turned_ref[width : width + 16].astype(F32)
    a, b = ids[0:1], ids[1:2]
    logits = gate_a[base : base + 16] + gate_b[base : base + 16]
    row = lax.broadcasted_iota(jnp.int32, logits.shape, 0).astype(F32)
    is_a, is_b = row == a, row == b
    la = jnp.sum(jnp.where(is_a, logits, 0.0), axis=0, keepdims=True)
    lb = jnp.sum(jnp.where(is_b, logits, 0.0), axis=0, keepdims=True)
    wa = 1.0 / (1.0 + jnp.exp(lb - la))
    wb = 1.0 / (1.0 + jnp.exp(la - lb))
    return (jnp.where(is_a, wa, 0.0) + jnp.where(is_b, wb, 0.0)).T


def down_terms(first, count, turned_ref, gate_a, gate_b, up_a, up_b, w_ref):
    experts, hidden, width = w_ref.shape
    factor = factors(turned_ref, gate_a, gate_b, width, experts * hidden, experts)
    total = None
    for i in range(count):
        e = first + i
        own = slice(e * hidden, (e + 1) * hidden)
        mine = slice(i * hidden, (i + 1) * hidden)
        gate = gate_a[own] + gate_b[own]
        up = up_a[mine] + up_b[mine]
        h = (gate / (1.0 + jnp.exp(-gate)) * up).T.astype(BF16)
        term = factor[:, e : e + 1] * jnp.dot(h, w_ref[e], preferred_element_type=F32)
        total = term if total is None else total + term
    return total


def down_first(count, turned_ref, gate_a, gate_b, up_a, up_b, w_ref, out_ref):
    out_ref[...] = down_terms(0, count, turned_ref, gate_a, gate_b, up_a, up_b, w_ref)


def down_last(first, count, turned_ref, gate_a, gate_b, up_a, up_b, w_ref, sum_ref, *outs):
    total = sum_ref[...] + down_terms(
        first, count, turned_ref, gate_a, gate_b, up_a, up_b, w_ref
    )
    rows = outs[0].shape[0]
    for j, out in enumerate(outs):
        out[...] = total[j * rows : (j + 1) * rows].astype(out.dtype)


def fast(tokens, expert_ids, router, w_gate, w_up, w_down):
    rows, width = tokens.shape
    experts, hidden, _ = w_gate.shape
    count = 8 * rows
    shape = lambda *s, dtype=F32: jax.ShapeDtypeStruct(s, dtype)
    (own,) = call(
        pack_kernel, [shape(rows, width + IDS, dtype=BF16)], [tokens, expert_ids], 0, 4 * rows * width, 1
    )
    far = xor_send(own, 4)
    near = [xor_send(own, k) for k in (1, 2, 3)]
    forwarded = [xor_send(far, k) for k in (1, 2, 3)]
    blocks = [own, *near, far, *forwarded]

    w_gate = pltpu.with_memory_space_constraint(w_gate, pltpu.HBM)
    w_up = pltpu.with_memory_space_constraint(w_up, pltpu.HBM)
    w_down = in_vmem(w_down)
    flops = 2 * count * hidden * width
    size = 2 * hidden * width
    slots, tile = 4, min(hidden, 256)
    held = [pltpu.VMEM((slots, tile, width), BF16), pltpu.SemaphoreType.DMA((slots,))]
    turned, gate = call(
        gate_kernel,
        [shape(width + IDS, count, dtype=BF16), shape(experts * hidden + 16, count)],
        [*blocks, jnp.pad(router.T, ((0, 16 - experts), (0, 0))), w_gate],
        experts * flops,
        experts * size,
        10,
        [pltpu.VMEM((count, width + IDS), F32), *held],
        hbm=(9,),
    )
    gate_other = lax.ppermute(gate, "mp", SWAP)
    half = experts // 2
    ups = []
    for first in (0, half):
        (up,) = call(
            functools.partial(up_kernel, range(first, first + half)),
            [shape(half * hidden, count)],
            [turned, w_up],
            half * flops,
            half * size,
            10,
            held,
            hbm=(1,),
        )
        ups.append((up, lax.ppermute(up, "mp", SWAP)))
    (partial_sum,) = call(
        functools.partial(down_first, half),
        [shape(count, width)],
        [turned, gate, gate_other, *ups[0], w_down],
        half * flops,
        half * size,
        8,
    )
    parts = call(
        functools.partial(down_last, half, half),
        [shape(rows, width)] + [shape(rows, width, dtype=BF16)] * 7,
        [turned, gate, gate_other, *ups[1], w_down, partial_sum],
        half * flops,
        half * size,
        8,
    )
    far_sums = [xor_send(parts[4 ^ k], k) for k in (1, 2, 3)]
    near_sums = [xor_send(parts[k], k) for k in (1, 2, 3)]
    add = lambda arrays: sum(a.astype(F32) for a in arrays)
    crossing = xor_send(add([parts[4], *far_sums]).astype(BF16), 4)
    return add([parts[0], *near_sums, crossing]).astype(BF16)


def general(tokens, expert_ids, router, w_gate, w_up, w_down):
    gathered, all_ids = (
        lax.all_gather(tokens, "batch", axis=0, tiled=True),
        lax.all_gather(expert_ids, "batch", axis=0, tiled=True),
    )
    token_count = gathered.shape[0]
    half_width = gathered.shape[1]
    experts = w_gate.shape[0]
    capacity = 3 * token_count // 4
    pair_expert = all_ids.reshape(-1)
    onehot = (pair_expert[:, None] == jnp.arange(experts, dtype=jnp.int32)[None, :]).astype(
        jnp.int32
    )
    position = jnp.sum((jnp.cumsum(onehot, axis=0) - 1) * onehot, axis=1)
    pair_token = jnp.arange(2 * token_count, dtype=jnp.int32) // 2
    slot_token = (
        jnp.full((experts, capacity), token_count, jnp.int32)
        .at[pair_expert, position]
        .set(pair_token)
    )
    slot_rows = jnp.take(gathered, jnp.minimum(slot_token, token_count - 1), axis=0)
    logit_part = jnp.dot(gathered, router, preferred_element_type=F32)
    gate_part = jnp.einsum("ecd,efd->ecf", slot_rows, w_gate, preferred_element_type=F32)
    up_part = jnp.einsum("ecd,efd->ecf", slot_rows, w_up, preferred_element_type=F32)
    logits, gate_sum, up_sum = lax.psum((logit_part, gate_part, up_part), "mp")
    chosen = jnp.take_along_axis(logits, all_ids, axis=1)
    weights = 1.0 / (1.0 + jnp.exp(chosen[:, ::-1] - chosen))
    slot_weight = (
        jnp.zeros((experts, capacity), F32)
        .at[pair_expert, position]
        .set(weights.reshape(-1))
    )
    hidden = (jax.nn.silu(gate_sum) * up_sum).astype(BF16)
    slot_out = (
        jnp.einsum("ecf,efd->ecd", hidden, w_down, preferred_element_type=F32)
        * slot_weight[:, :, None]
    )
    partial_value = (
        jnp.zeros((token_count, half_width), F32)
        .at[slot_token.reshape(-1)]
        .add(slot_out.reshape(-1, half_width), mode="drop")
    )
    mine = lax.psum_scatter(partial_value, "batch", scatter_dimension=0, tiled=True)
    return mine.astype(BF16)


def solution(mesh):
    def per_device(*args):
        rows, (experts, hidden, _) = args[0].shape[0], args[3].shape
        fits = mesh.shape["batch"] == 8 and rows % 16 == 0 and 8 * rows <= 128
        if fits and experts == 4 and hidden <= 1024:
            return fast(*args)
        return general(*args)

    in_specs = (
        P(("group", "batch"), "mp"),
        P(("group", "batch"), None),
        P("mp", None),
        P(None, "batch", "mp"),
        P(None, "batch", "mp"),
        P(None, "batch", "mp"),
    )
    out_specs = P(("group", "batch"), "mp")
    return jax.shard_map(
        per_device, mesh=mesh, in_specs=in_specs, out_specs=out_specs, check_vma=False
    )
```

```python
import functools
import jax
import jax.numpy as jnp
from jax import lax
from jax.experimental import pallas as pl
from jax.experimental.pallas import tpu as pltpu
from jax.sharding import PartitionSpec as P

F32, BF16 = jnp.float32, jnp.bfloat16
IDS = 128
SWAP = [(0, 1), (1, 0)]
HBM_BLOCK = pl.BlockSpec(memory_space=pltpu.HBM)
VMEM_BLOCK = pl.BlockSpec(memory_space=pltpu.VMEM)


def xor_send(block, mask):
    return lax.ppermute(block, "batch", [(i, i ^ mask) for i in range(8)])


def in_vmem(array):
    return pltpu.with_memory_space_constraint(array, pltpu.VMEM)


def call(kernel, outs, args, flops, size, vmem, scratch=(), hbm=()):
    specs = [HBM_BLOCK if i in hbm else VMEM_BLOCK for i in range(len(args))]
    return pl.pallas_call(
        kernel,
        out_shape=outs,
        in_specs=specs,
        out_specs=[VMEM_BLOCK] * len(outs),
        scratch_shapes=list(scratch),
        compiler_params=pltpu.CompilerParams(vmem_limit_bytes=int(vmem * 2**20)),
        cost_estimate=pl.CostEstimate(flops=flops, bytes_accessed=size, transcendentals=0),
    )(*args)


def pack_kernel(tokens_ref, ids_ref, out_ref):
    rows, width = tokens_ref.shape
    out_ref[:, :width] = tokens_ref[...]
    ids = ids_ref[...].astype(F32)
    lane = lax.broadcasted_iota(jnp.int32, (rows, IDS), 1)
    out_ref[:, width:] = jnp.where(lane == 0, ids[:, 0:1], ids[:, 1:2]).astype(BF16)


def stream(w_ref, held_ref, sems, experts, part_ref, load):
    hidden, width = w_ref.shape[1:]
    slots, tile = held_ref.shape[:2]
    steps = [(e, f) for e in experts for f in range(0, hidden, tile)]

    def copy(step):
        e, f = steps[step]
        slot = step % slots
        return pltpu.make_async_copy(
            w_ref.at[e, pl.ds(f, tile)], held_ref.at[slot], sems.at[slot]
        )

    for step in range(min(slots, len(steps))):
        copy(step).start()
    x = load()
    for step in range(len(steps)):
        copy(step).wait()
        part_ref[step * tile : (step + 1) * tile] = jnp.dot(
            held_ref[step % slots], x, preferred_element_type=F32
        )
        if step + slots < len(steps):
            copy(step + slots).start()


def gate_kernel(*refs):
    blocks, (router_ref, w_ref, turned_ref, part_ref) = refs[:8], refs[8:12]
    rows_ref, held_ref, sems = refs[12:]
    experts, hidden, width = w_ref.shape

    def load():
        rows = blocks[0].shape[0]
        for j, block in enumerate(blocks):
            rows_ref[j * rows : (j + 1) * rows] = block[...].astype(F32)
        turned_ref[...] = rows_ref[...].T.astype(BF16)
        x = turned_ref[:width]
        part_ref[experts * hidden :] = jnp.dot(
            router_ref[...], x, preferred_element_type=F32
        )
        return x

    stream(w_ref, held_ref, sems, range(experts), part_ref, load)


def up_kernel(experts, turned_ref, w_ref, _, part_ref, sent_ref, held_ref, sems):
    width = w_ref.shape[2]
    stream(w_ref, held_ref, sems, experts, part_ref, lambda: turned_ref[:width])
    sent_ref[...] = part_ref[...].astype(BF16)


def factors(turned_ref, gate_a, gate_b, width, base, experts):
    ids = turned_ref[width : width + 16].astype(F32)
    a, b = ids[0:1], ids[1:2]
    logits = gate_a[base : base + 16] + gate_b[base : base + 16]
    row = lax.broadcasted_iota(jnp.int32, logits.shape, 0).astype(F32)
    is_a, is_b = row == a, row == b
    la = jnp.sum(jnp.where(is_a, logits, 0.0), axis=0, keepdims=True)
    lb = jnp.sum(jnp.where(is_b, logits, 0.0), axis=0, keepdims=True)
    wa = 1.0 / (1.0 + jnp.exp(lb - la))
    wb = 1.0 / (1.0 + jnp.exp(la - lb))
    return (jnp.where(is_a, wa, 0.0) + jnp.where(is_b, wb, 0.0)).T


def hidden_units(e, i, hidden, gate_a, gate_b, up_a, up_b):
    own = slice(e * hidden, (e + 1) * hidden)
    mine = slice(i * hidden, (i + 1) * hidden)
    gate = gate_a[own] + gate_b[own]
    up = up_a[mine] + up_b[mine].astype(F32)
    return (gate / (1.0 + jnp.exp(-gate)) * up).T.astype(BF16)


def hidden_kernel(experts, gate_a, gate_b, up_a, up_b, _, out_ref):
    hidden = out_ref.shape[2]
    for i, e in enumerate(experts):
        out_ref[i] = hidden_units(e, i, hidden, gate_a, gate_b, up_a, up_b)


def down_kernel(first, turned_ref, gate_a, gate_b, up_a, up_b, h_ref, w_ref, *outs):
    experts, hidden, width = w_ref.shape
    factor = factors(turned_ref, gate_a, gate_b, width, experts * hidden, experts)
    total = None
    for e in range(experts):
        if e < first:
            h = h_ref[e]
        else:
            h = hidden_units(e, e - first, hidden, gate_a, gate_b, up_a, up_b)
        term = factor[:, e : e + 1] * jnp.dot(h, w_ref[e], preferred_element_type=F32)
        total = term if total is None else total + term
    rows = outs[0].shape[0]
    for j, out in enumerate(outs):
        out[...] = total[j * rows : (j + 1) * rows].astype(out.dtype)


def fast(tokens, expert_ids, router, w_gate, w_up, w_down):
    rows, width = tokens.shape
    experts, hidden, _ = w_gate.shape
    count = 8 * rows
    shape = lambda *s, dtype=F32: jax.ShapeDtypeStruct(s, dtype)
    (own,) = call(
        pack_kernel, [shape(rows, width + IDS, dtype=BF16)], [tokens, expert_ids], 0, 4 * rows * width, 1
    )
    far = xor_send(own, 4)
    near = [xor_send(own, k) for k in (1, 2, 3)]
    forwarded = [xor_send(far, k) for k in (1, 2, 3)]
    blocks = [own, *near, far, *forwarded]

    w_gate = pltpu.with_memory_space_constraint(w_gate, pltpu.HBM)
    w_up = pltpu.with_memory_space_constraint(w_up, pltpu.HBM)
    w_down = in_vmem(w_down)
    flops = 2 * count * hidden * width
    size = 2 * hidden * width
    slots, tile = 3, min(hidden, 256)
    held = [pltpu.VMEM((slots, tile, width), BF16), pltpu.SemaphoreType.DMA((slots,))]
    turned, gate = call(
        gate_kernel,
        [shape(width + IDS, count, dtype=BF16), shape(experts * hidden + 16, count)],
        [*blocks, jnp.pad(router.T, ((0, 16 - experts), (0, 0))), w_gate],
        experts * flops,
        experts * size,
        8,
        [pltpu.VMEM((count, width + IDS), F32), *held],
        hbm=(9,),
    )
    gate_other = lax.ppermute(gate, "mp", SWAP)
    half = experts // 2
    ups = []
    for first in (0, half):
        up, sent = call(
            functools.partial(up_kernel, range(first, first + half)),
            [shape(half * hidden, count), shape(half * hidden, count, dtype=BF16)],
            [turned, w_up, w_down],
            half * flops,
            half * size,
            8,
            held,
            hbm=(1,),
        )
        ups.append((up, lax.ppermute(sent, "mp", SWAP)))
    (units,) = call(
        functools.partial(hidden_kernel, range(half)),
        [shape(half, count, hidden, dtype=BF16)],
        [gate, gate_other, *ups[0], w_down],
        0,
        12 * half * hidden * count,
        4,
    )
    parts = call(
        functools.partial(down_kernel, half),
        [shape(rows, width)] + [shape(rows, width, dtype=BF16)] * 7,
        [turned, gate, gate_other, *ups[1], units, w_down],
        experts * flops,
        experts * size,
        5,
    )
    far_sums = [xor_send(parts[4 ^ k], k) for k in (1, 2, 3)]
    near_sums = [xor_send(parts[k], k) for k in (1, 2, 3)]
    add = lambda arrays: sum(a.astype(F32) for a in arrays)
    crossing = xor_send(add([parts[4], *far_sums]).astype(BF16), 4)
    return add([parts[0], *near_sums, crossing]).astype(BF16)


def general(tokens, expert_ids, router, w_gate, w_up, w_down):
    gathered, all_ids = (
        lax.all_gather(tokens, "batch", axis=0, tiled=True),
        lax.all_gather(expert_ids, "batch", axis=0, tiled=True),
    )
    token_count = gathered.shape[0]
    half_width = gathered.shape[1]
    experts = w_gate.shape[0]
    capacity = 3 * token_count // 4
    pair_expert = all_ids.reshape(-1)
    onehot = (pair_expert[:, None] == jnp.arange(experts, dtype=jnp.int32)[None, :]).astype(
        jnp.int32
    )
    position = jnp.sum((jnp.cumsum(onehot, axis=0) - 1) * onehot, axis=1)
    pair_token = jnp.arange(2 * token_count, dtype=jnp.int32) // 2
    slot_token = (
        jnp.full((experts, capacity), token_count, jnp.int32)
        .at[pair_expert, position]
        .set(pair_token)
    )
    slot_rows = jnp.take(gathered, jnp.minimum(slot_token, token_count - 1), axis=0)
    logit_part = jnp.dot(gathered, router, preferred_element_type=F32)
    gate_part = jnp.einsum("ecd,efd->ecf", slot_rows, w_gate, preferred_element_type=F32)
    up_part = jnp.einsum("ecd,efd->ecf", slot_rows, w_up, preferred_element_type=F32)
    logits, gate_sum, up_sum = lax.psum((logit_part, gate_part, up_part), "mp")
    chosen = jnp.take_along_axis(logits, all_ids, axis=1)
    weights = 1.0 / (1.0 + jnp.exp(chosen[:, ::-1] - chosen))
    slot_weight = (
        jnp.zeros((experts, capacity), F32)
        .at[pair_expert, position]
        .set(weights.reshape(-1))
    )
    hidden = (jax.nn.silu(gate_sum) * up_sum).astype(BF16)
    slot_out = (
        jnp.einsum("ecf,efd->ecd", hidden, w_down, preferred_element_type=F32)
        * slot_weight[:, :, None]
    )
    partial_value = (
        jnp.zeros((token_count, half_width), F32)
        .at[slot_token.reshape(-1)]
        .add(slot_out.reshape(-1, half_width), mode="drop")
    )
    mine = lax.psum_scatter(partial_value, "batch", scatter_dimension=0, tiled=True)
    return mine.astype(BF16)


def solution(mesh):
    def per_device(*args):
        rows, (experts, hidden, _) = args[0].shape[0], args[3].shape
        fits = mesh.shape["batch"] == 8 and rows % 16 == 0 and 8 * rows <= 128
        if fits and experts == 4 and hidden <= 1024:
            return fast(*args)
        return general(*args)

    in_specs = (
        P(("group", "batch"), "mp"),
        P(("group", "batch"), None),
        P("mp", None),
        P(None, "batch", "mp"),
        P(None, "batch", "mp"),
        P(None, "batch", "mp"),
    )
    out_specs = P(("group", "batch"), "mp")
    return jax.shard_map(
        per_device, mesh=mesh, in_specs=in_specs, out_specs=out_specs, check_vma=False
    )
```

```python
import functools
import jax
import jax.numpy as jnp
from jax import lax
from jax.experimental import pallas as pl
from jax.experimental.pallas import tpu as pltpu
from jax.sharding import PartitionSpec as P

F32, BF16 = jnp.float32, jnp.bfloat16
IDS = 128
SWAP = [(0, 1), (1, 0)]
HBM_BLOCK = pl.BlockSpec(memory_space=pltpu.HBM)
VMEM_BLOCK = pl.BlockSpec(memory_space=pltpu.VMEM)


def xor_send(block, mask):
    return lax.ppermute(block, "batch", [(i, i ^ mask) for i in range(8)])


def in_vmem(array):
    return pltpu.with_memory_space_constraint(array, pltpu.VMEM)


def call(kernel, outs, args, flops, size, vmem, scratch=(), hbm=()):
    specs = [HBM_BLOCK if i in hbm else VMEM_BLOCK for i in range(len(args))]
    return pl.pallas_call(
        kernel,
        out_shape=outs,
        in_specs=specs,
        out_specs=[VMEM_BLOCK] * len(outs),
        scratch_shapes=list(scratch),
        compiler_params=pltpu.CompilerParams(vmem_limit_bytes=int(vmem * 2**20)),
        cost_estimate=pl.CostEstimate(flops=flops, bytes_accessed=size, transcendentals=0),
    )(*args)


def column(row, rows):
    diagonal = lax.broadcasted_iota(jnp.int32, (rows, rows), 0) == lax.broadcasted_iota(
        jnp.int32, (rows, rows), 1
    )
    return jnp.sum(jnp.where(diagonal, row, 0.0), axis=1, keepdims=True)


def pack_kernel(tokens_ref, ids_ref, out_ref):
    rows, width = tokens_ref.shape
    out_ref[:, :width] = tokens_ref[...]
    ids = ids_ref[...].astype(F32)
    lane = lax.broadcasted_iota(jnp.int32, (rows, IDS), 1)
    out_ref[:, width:] = jnp.where(
        lane == 0, column(ids[0:1], rows), column(ids[1:2], rows)
    ).astype(BF16)


def over_width(a, b):
    return lax.dot_general(a, b, (((1,), (1,)), ((), ())), preferred_element_type=F32)


def fetch_kernel(_, source_ref, out_ref, sems):
    copies = [
        pltpu.make_async_copy(source_ref.at[i], out_ref.at[i], sems.at[i])
        for i in range(out_ref.shape[0])
    ]
    for copy in copies:
        copy.start()
    for copy in copies:
        copy.wait()


def stream(steps, held_ref, sems, x, first):
    slots, tile = held_ref.shape[:2]

    def copy(step):
        w_ref, e, f, _ = steps[step]
        slot = step % slots
        return pltpu.make_async_copy(
            w_ref.at[e, pl.ds(f, tile)], held_ref.at[slot], sems.at[slot]
        )

    for step in range(slots):
        copy(step).start()
    first()
    for step, (*_, store) in enumerate(steps):
        copy(step).wait()
        store(over_width(held_ref[step % slots], x))
        if step + slots < len(steps):
            copy(step + slots).start()


def up_store(part_ref, sent_ref, at):
    def store(part):
        own = slice(at, at + part.shape[0])
        part_ref[own] = part
        sent_ref[own] = part.astype(BF16)

    return store


def gate_store(part_ref, at):
    def store(part):
        part_ref[at : at + part.shape[0]] = part

    return store


def gate_kernel(*refs):
    blocks, refs = refs[:8], refs[8:]
    router_ref, early_ref, gate_ref, up_ref, x_ref, part_ref, up_part, up_sent, *scratch = refs
    held_ref, sems = scratch
    experts, hidden, width = gate_ref.shape
    tile = held_ref.shape[1]
    early, half = early_ref.shape[0], experts // 2
    rows = blocks[0].shape[0]
    for j, block in enumerate(blocks):
        x_ref[j * rows : (j + 1) * rows] = block[...]
    x = x_ref[:, :width]

    def first():
        part_ref[experts * hidden :] = over_width(x, router_ref[...])
        for e in range(early):
            part_ref[e * hidden : (e + 1) * hidden] = over_width(early_ref[e], x)

    steps = [
        (gate_ref, e, f, gate_store(part_ref, e * hidden + f))
        for e in range(early, experts)
        for f in range(0, hidden, tile)
    ] + [
        (up_ref, e, f, up_store(up_part, up_sent, e * hidden + f))
        for e in range(half)
        for f in range(0, hidden, tile)
    ]
    stream(steps, held_ref, sems, x, first)


def up_kernel(x_ref, up_ref, _, part_ref, sent_ref, held_ref, sems):
    experts, hidden, width = up_ref.shape
    tile, half = held_ref.shape[1], experts // 2
    steps = [
        (up_ref, half + i, f, up_store(part_ref, sent_ref, i * hidden + f))
        for i in range(half)
        for f in range(0, hidden, tile)
    ]
    stream(steps, held_ref, sems, x_ref[:, :width], lambda: None)


def factors(x_ref, gate_a, gate_b, width, base):
    count = x_ref.shape[0]
    ids = x_ref[:, width:].astype(F32)
    a, b = ids[:, 0:1], ids[:, 1:2]
    logits = gate_a[base : base + count] + gate_b[base : base + count]
    lane = lax.broadcasted_iota(jnp.int32, logits.shape, 1).astype(F32)
    is_a, is_b = lane == a, lane == b
    la = jnp.sum(jnp.where(is_a, logits, 0.0), axis=1, keepdims=True)
    lb = jnp.sum(jnp.where(is_b, logits, 0.0), axis=1, keepdims=True)
    wa = 1.0 / (1.0 + jnp.exp(lb - la))
    wb = 1.0 / (1.0 + jnp.exp(la - lb))
    return jnp.where(is_a, wa, 0.0) + jnp.where(is_b, wb, 0.0)


def hidden_units(e, i, hidden, gate_a, gate_b, up_a, up_b):
    own = slice(e * hidden, (e + 1) * hidden)
    mine = slice(i * hidden, (i + 1) * hidden)
    gate = gate_a[own] + gate_b[own]
    up = up_a[mine] + up_b[mine].astype(F32)
    return (gate / (1.0 + jnp.exp(-gate)) * up).T.astype(BF16)


def hidden_kernel(experts, gate_a, gate_b, up_a, up_b, _, out_ref):
    hidden = out_ref.shape[2]
    for i, e in enumerate(experts):
        out_ref[i] = hidden_units(e, i, hidden, gate_a, gate_b, up_a, up_b)


def down_kernel(x_ref, gate_a, gate_b, up_a, up_b, h_ref, w_ref, *outs):
    experts, hidden, width = w_ref.shape
    half = h_ref.shape[0]
    factor = factors(x_ref, gate_a, gate_b, width, experts * hidden)
    total = None
    for e in range(experts):
        if e < half:
            h = h_ref[e]
        else:
            h = hidden_units(e, e - half, hidden, gate_a, gate_b, up_a, up_b)
        term = factor[:, e : e + 1] * jnp.dot(h, w_ref[e], preferred_element_type=F32)
        total = term if total is None else total + term
    rows = outs[0].shape[0]
    for j, out in enumerate(outs):
        out[...] = total[j * rows : (j + 1) * rows].astype(out.dtype)


def fast(tokens, expert_ids, router, w_gate, w_up, w_down):
    rows, width = tokens.shape
    experts, hidden, _ = w_gate.shape
    count, half = 8 * rows, experts // 2
    shape = lambda *s, dtype=F32: jax.ShapeDtypeStruct(s, dtype)
    (own,) = call(
        pack_kernel,
        [shape(rows, width + IDS, dtype=BF16)],
        [tokens, expert_ids.T],
        0,
        4 * rows * width,
        1,
    )
    far = xor_send(own, 4)
    near = [xor_send(own, k) for k in (1, 2, 3)]
    forwarded = [xor_send(far, k) for k in (1, 2, 3)]
    blocks = [own, *near, far, *forwarded]

    in_hbm = lambda array: pltpu.with_memory_space_constraint(array, pltpu.HBM)
    w_gate, w_up, w_down = in_hbm(w_gate), in_hbm(w_up), in_vmem(w_down)
    flops = 2 * count * hidden * width
    size = 2 * hidden * width
    lines = jnp.pad(router.T, ((0, 128 - experts), (0, 0)))
    slots, tile, early = 4, min(hidden, 256), 2
    held = [pltpu.VMEM((slots, tile, width), BF16), pltpu.SemaphoreType.DMA((slots,))]
    (w_early,) = call(
        fetch_kernel,
        [pltpu.VMEM((early, hidden, width), BF16)],
        [far[:, :128], w_gate],
        0,
        0,
        1,
        [pltpu.SemaphoreType.DMA((early,))],
        hbm=(1,),
    )
    up_shapes = [shape(half * hidden, count), shape(half * hidden, count, dtype=BF16)]
    x, gate, up_a, sent_a = call(
        gate_kernel,
        [
            shape(count, width + IDS, dtype=BF16),
            shape(experts * hidden + count, count),
            *up_shapes,
        ],
        [*blocks, lines, w_early, w_gate, w_up],
        experts * flops,
        experts * size,
        8,
        held,
        hbm=(10, 11),
    )
    gate_other = lax.ppermute(gate, "mp", SWAP)
    up_other_a = lax.ppermute(sent_a, "mp", SWAP)
    up_b, sent_b = call(
        up_kernel, up_shapes, [x, w_up, w_down], half * flops, half * size, 7, held, hbm=(1,)
    )
    up_other_b = lax.ppermute(sent_b, "mp", SWAP)
    (units,) = call(
        functools.partial(hidden_kernel, range(half)),
        [shape(half, count, hidden, dtype=BF16)],
        [gate, gate_other, up_a, up_other_a, w_down],
        0,
        12 * half * hidden * count,
        4,
    )
    parts = call(
        down_kernel,
        [shape(rows, width)] + [shape(rows, width, dtype=BF16)] * 7,
        [x, gate, gate_other, up_b, up_other_b, units, w_down],
        experts * flops,
        experts * size,
        5,
    )
    add = lambda arrays: sum(a.astype(F32) for a in arrays)
    far_sums = [xor_send(parts[4 ^ k], k) for k in (3, 2, 1)]
    leaving, *kept = lax.optimization_barrier(
        (add([parts[4], *far_sums]).astype(BF16), *parts[1:4])
    )
    near_sums = [xor_send(kept[k - 1], k) for k in (3, 2, 1)]
    crossing = xor_send(leaving, 4)
    return add([parts[0], crossing, *near_sums]).astype(BF16)


def general(tokens, expert_ids, router, w_gate, w_up, w_down):
    gathered, all_ids = (
        lax.all_gather(tokens, "batch", axis=0, tiled=True),
        lax.all_gather(expert_ids, "batch", axis=0, tiled=True),
    )
    token_count = gathered.shape[0]
    half_width = gathered.shape[1]
    experts = w_gate.shape[0]
    capacity = 3 * token_count // 4
    pair_expert = all_ids.reshape(-1)
    onehot = (pair_expert[:, None] == jnp.arange(experts, dtype=jnp.int32)[None, :]).astype(
        jnp.int32
    )
    position = jnp.sum((jnp.cumsum(onehot, axis=0) - 1) * onehot, axis=1)
    pair_token = jnp.arange(2 * token_count, dtype=jnp.int32) // 2
    slot_token = (
        jnp.full((experts, capacity), token_count, jnp.int32)
        .at[pair_expert, position]
        .set(pair_token)
    )
    slot_rows = jnp.take(gathered, jnp.minimum(slot_token, token_count - 1), axis=0)
    logit_part = jnp.dot(gathered, router, preferred_element_type=F32)
    gate_part = jnp.einsum("ecd,efd->ecf", slot_rows, w_gate, preferred_element_type=F32)
    up_part = jnp.einsum("ecd,efd->ecf", slot_rows, w_up, preferred_element_type=F32)
    logits, gate_sum, up_sum = lax.psum((logit_part, gate_part, up_part), "mp")
    chosen = jnp.take_along_axis(logits, all_ids, axis=1)
    weights = 1.0 / (1.0 + jnp.exp(chosen[:, ::-1] - chosen))
    slot_weight = (
        jnp.zeros((experts, capacity), F32)
        .at[pair_expert, position]
        .set(weights.reshape(-1))
    )
    hidden = (jax.nn.silu(gate_sum) * up_sum).astype(BF16)
    slot_out = (
        jnp.einsum("ecf,efd->ecd", hidden, w_down, preferred_element_type=F32)
        * slot_weight[:, :, None]
    )
    partial_value = (
        jnp.zeros((token_count, half_width), F32)
        .at[slot_token.reshape(-1)]
        .add(slot_out.reshape(-1, half_width), mode="drop")
    )
    mine = lax.psum_scatter(partial_value, "batch", scatter_dimension=0, tiled=True)
    return mine.astype(BF16)


def solution(mesh):
    def per_device(*args):
        rows, (experts, hidden, _) = args[0].shape[0], args[3].shape
        fits = mesh.shape["batch"] == 8 and rows % 16 == 0 and 8 * rows <= 128
        if fits and experts == 4 and hidden <= 1024:
            return fast(*args)
        return general(*args)

    in_specs = (
        P(("group", "batch"), "mp"),
        P(("group", "batch"), None),
        P("mp", None),
        P(None, "batch", "mp"),
        P(None, "batch", "mp"),
        P(None, "batch", "mp"),
    )
    out_specs = P(("group", "batch"), "mp")
    return jax.shard_map(
        per_device, mesh=mesh, in_specs=in_specs, out_specs=out_specs, check_vma=False
    )
```

```python
import functools
import jax
import jax.numpy as jnp
from jax import lax
from jax.experimental import pallas as pl
from jax.experimental.pallas import tpu as pltpu
from jax.sharding import PartitionSpec as P

F32, BF16 = jnp.float32, jnp.bfloat16
IDS = 128
SWAP = [(0, 1), (1, 0)]
HBM_BLOCK = pl.BlockSpec(memory_space=pltpu.HBM)
VMEM_BLOCK = pl.BlockSpec(memory_space=pltpu.VMEM)


def xor_send(block, mask):
    return lax.ppermute(block, "batch", [(i, i ^ mask) for i in range(8)])


def in_vmem(array):
    return pltpu.with_memory_space_constraint(array, pltpu.VMEM)


def call(kernel, outs, args, flops, size, vmem, scratch=(), hbm=()):
    specs = [HBM_BLOCK if i in hbm else VMEM_BLOCK for i in range(len(args))]
    return pl.pallas_call(
        kernel,
        out_shape=outs,
        in_specs=specs,
        out_specs=[VMEM_BLOCK] * len(outs),
        scratch_shapes=list(scratch),
        compiler_params=pltpu.CompilerParams(vmem_limit_bytes=int(vmem * 2**20)),
        cost_estimate=pl.CostEstimate(flops=flops, bytes_accessed=size, transcendentals=0),
    )(*args)


def column(row, rows):
    diagonal = lax.broadcasted_iota(jnp.int32, (rows, rows), 0) == lax.broadcasted_iota(
        jnp.int32, (rows, rows), 1
    )
    return jnp.sum(jnp.where(diagonal, row, 0.0), axis=1, keepdims=True)


def pack_kernel(tokens_ref, ids_ref, out_ref):
    rows, width = tokens_ref.shape
    out_ref[:, :width] = tokens_ref[...]
    ids = ids_ref[...].astype(F32)
    lane = lax.broadcasted_iota(jnp.int32, (rows, IDS), 1)
    out_ref[:, width:] = jnp.where(
        lane == 0, column(ids[0:1], rows), column(ids[1:2], rows)
    ).astype(BF16)


def over_width(a, b):
    return lax.dot_general(a, b, (((1,), (1,)), ((), ())), preferred_element_type=F32)


def fetches(source_ref, experts, targets, sems, at=0):
    return [
        pltpu.make_async_copy(source_ref.at[e], target, sems.at[at + i])
        for i, (e, target) in enumerate(zip(experts, targets))
    ]


def fetch_kernel(fetched, _, source_ref, *refs):
    *held, sems = refs
    copies = fetches(source_ref, fetched, held, sems)
    for copy in copies:
        copy.start()
    for copy in copies:
        copy.wait()


def gate_kernel(fetched, *refs):
    blocks, (router_ref, w_ref, up_ref, _, x_ref, part_ref, *held, sems) = refs[:8], refs[8:]
    experts, hidden, width = w_ref.shape
    copies = fetches(up_ref, fetched, held, sems)
    for copy in copies:
        copy.start()
    rows = blocks[0].shape[0]
    for j, block in enumerate(blocks):
        x_ref[j * rows : (j + 1) * rows] = block[...]
    x = x_ref[:, :width]
    part_ref[experts * hidden :] = over_width(x, router_ref[...])
    for e in range(experts):
        part_ref[e * hidden : (e + 1) * hidden] = over_width(w_ref[e], x)
    for copy in copies:
        copy.wait()


def up_kernel(up_fetched, down_fetched, x_ref, up_ref, down_ref, *refs):
    weights, (part_ref, sent_ref, *held, sems) = refs[:2], refs[2:]
    hidden, width = weights[0].shape
    n = len(up_fetched)
    copies = fetches(up_ref, up_fetched, held[:n], sems) + fetches(
        down_ref, down_fetched, held[n:], sems, n
    )
    for copy in copies:
        copy.start()
    x = x_ref[:, :width]
    for i, w_ref in enumerate(weights):
        own = slice(i * hidden, (i + 1) * hidden)
        part = over_width(w_ref[...], x)
        part_ref[own] = part
        sent_ref[own] = part.astype(BF16)
    for copy in copies:
        copy.wait()


def factors(x_ref, gate_a, gate_b, width, base):
    count = x_ref.shape[0]
    ids = x_ref[:, width:].astype(F32)
    a, b = ids[:, 0:1], ids[:, 1:2]
    logits = gate_a[base : base + count] + gate_b[base : base + count]
    lane = lax.broadcasted_iota(jnp.int32, logits.shape, 1).astype(F32)
    is_a, is_b = lane == a, lane == b
    la = jnp.sum(jnp.where(is_a, logits, 0.0), axis=1, keepdims=True)
    lb = jnp.sum(jnp.where(is_b, logits, 0.0), axis=1, keepdims=True)
    wa = 1.0 / (1.0 + jnp.exp(lb - la))
    wb = 1.0 / (1.0 + jnp.exp(la - lb))
    return jnp.where(is_a, wa, 0.0) + jnp.where(is_b, wb, 0.0)


def hidden_units(e, i, hidden, gate_a, gate_b, up_a, up_b):
    own = slice(e * hidden, (e + 1) * hidden)
    mine = slice(i * hidden, (i + 1) * hidden)
    gate = gate_a[own] + gate_b[own]
    up = up_a[mine] + up_b[mine].astype(F32)
    return (gate / (1.0 + jnp.exp(-gate)) * up).T.astype(BF16)


def hidden_kernel(experts, fetched, gate_a, gate_b, up_a, up_b, down_ref, out_ref, *refs):
    *held, sems = refs
    copies = fetches(down_ref, fetched, held, sems)
    for copy in copies:
        copy.start()
    hidden = out_ref.shape[2]
    for i, e in enumerate(experts):
        out_ref[i] = hidden_units(e, i, hidden, gate_a, gate_b, up_a, up_b)
    for copy in copies:
        copy.wait()


def down_kernel(ready, x_ref, gate_a, gate_b, up_a, up_b, h_ref, down_ref, *refs):
    weights, outs, (held_ref, sems) = refs[:ready], refs[ready : ready + 8], refs[ready + 8 :]
    experts, hidden, width = down_ref.shape
    late = [held_ref.at[i] for i in range(experts - ready)]
    copies = fetches(down_ref, range(ready, experts), late, sems)
    for copy in copies:
        copy.start()
    half = h_ref.shape[0]
    factor = factors(x_ref, gate_a, gate_b, width, experts * hidden)
    total = None
    for e in range(experts):
        if e < half:
            h = h_ref[e]
        else:
            h = hidden_units(e, e - half, hidden, gate_a, gate_b, up_a, up_b)
        if e < ready:
            w = weights[e][...]
        else:
            copies[e - ready].wait()
            w = late[e - ready][...]
        term = factor[:, e : e + 1] * jnp.dot(h, w, preferred_element_type=F32)
        total = term if total is None else total + term
    rows = outs[0].shape[0]
    for j, out in enumerate(outs):
        out[...] = total[j * rows : (j + 1) * rows].astype(out.dtype)


def fast(tokens, expert_ids, router, w_gate, w_up, w_down):
    rows, width = tokens.shape
    experts, hidden, _ = w_gate.shape
    count, half = 8 * rows, experts // 2
    shape = lambda *s, dtype=F32: jax.ShapeDtypeStruct(s, dtype)
    (own,) = call(
        pack_kernel,
        [shape(rows, width + IDS, dtype=BF16)],
        [tokens, expert_ids.T],
        30_000_000_000,
        4 * rows * width,
        1,
    )
    far = xor_send(own, 4)
    near = [xor_send(own, k) for k in (1, 2, 3)]
    forwarded = [xor_send(far, k) for k in (1, 2, 3)]
    blocks = [own, *near, far, *forwarded]

    in_hbm = lambda array: pltpu.with_memory_space_constraint(array, pltpu.HBM)
    w_gate, w_up, w_down = in_vmem(w_gate), in_hbm(w_up), in_hbm(w_down)
    flops = 2 * count * hidden * width
    size = 2 * hidden * width
    lines = jnp.pad(router.T, ((0, 128 - experts), (0, 0)))
    one = pltpu.VMEM((hidden, width), BF16)
    sems = lambda n: [pltpu.SemaphoreType.DMA((n,))]
    (up0,) = call(
        functools.partial(fetch_kernel, (0,)),
        [one],
        [far[:, :128], w_up],
        14_000_000_000,
        0,
        1,
        sems(1),
        hbm=(1,),
    )
    x, gate, up1, up2 = call(
        functools.partial(gate_kernel, (1, 2)),
        [
            shape(count, width + IDS, dtype=BF16),
            shape(experts * hidden + count, count),
            *[one] * 2,
        ],
        [*blocks, lines, w_gate, w_up, up0],
        experts * flops,
        experts * size,
        3,
        sems(2),
        hbm=(10,),
    )
    gate_other = lax.ppermute(gate, "mp", SWAP)

    def up_call(up_fetched, down_fetched, weights):
        n = len(up_fetched) + len(down_fetched)
        part, sent, *held = call(
            functools.partial(up_kernel, up_fetched, down_fetched),
            [
                shape(half * hidden, count),
                shape(half * hidden, count, dtype=BF16),
                *[one] * n,
            ],
            [x, w_up, w_down, *weights],
            half * flops,
            half * size,
            3,
            sems(n),
            hbm=(1, 2),
        )
        return (part, lax.ppermute(sent, "mp", SWAP)), held

    first, (up3,) = up_call((3,), (), (up0, up1))
    second, (down0, down1) = up_call((), (0, 1), (up2, up3))
    units, down2 = call(
        functools.partial(hidden_kernel, range(half), (2,)),
        [shape(half, count, hidden, dtype=BF16), one],
        [gate, gate_other, *first, w_down],
        0,
        12 * half * hidden * count,
        4,
        sems(1),
        hbm=(4,),
    )
    parts = call(
        functools.partial(down_kernel, 3),
        [shape(rows, width)] + [shape(rows, width, dtype=BF16)] * 7,
        [x, gate, gate_other, *second, units, w_down, down0, down1, down2],
        experts * flops,
        experts * size,
        10,
        [pltpu.VMEM((1, hidden, width), BF16), *sems(1)],
        hbm=(6,),
    )
    far_sums = [xor_send(parts[4 ^ k], k) for k in (1, 2, 3)]
    near_sums = [xor_send(parts[k], k) for k in (1, 2, 3)]
    add = lambda arrays: sum(a.astype(F32) for a in arrays)
    crossing = xor_send(add([parts[4], *far_sums]).astype(BF16), 4)
    return add([parts[0], *near_sums, crossing]).astype(BF16)


def general(tokens, expert_ids, router, w_gate, w_up, w_down):
    gathered, all_ids = (
        lax.all_gather(tokens, "batch", axis=0, tiled=True),
        lax.all_gather(expert_ids, "batch", axis=0, tiled=True),
    )
    token_count = gathered.shape[0]
    half_width = gathered.shape[1]
    experts = w_gate.shape[0]
    capacity = 3 * token_count // 4
    pair_expert = all_ids.reshape(-1)
    onehot = (pair_expert[:, None] == jnp.arange(experts, dtype=jnp.int32)[None, :]).astype(
        jnp.int32
    )
    position = jnp.sum((jnp.cumsum(onehot, axis=0) - 1) * onehot, axis=1)
    pair_token = jnp.arange(2 * token_count, dtype=jnp.int32) // 2
    slot_token = (
        jnp.full((experts, capacity), token_count, jnp.int32)
        .at[pair_expert, position]
        .set(pair_token)
    )
    slot_rows = jnp.take(gathered, jnp.minimum(slot_token, token_count - 1), axis=0)
    logit_part = jnp.dot(gathered, router, preferred_element_type=F32)
    gate_part = jnp.einsum("ecd,efd->ecf", slot_rows, w_gate, preferred_element_type=F32)
    up_part = jnp.einsum("ecd,efd->ecf", slot_rows, w_up, preferred_element_type=F32)
    logits, gate_sum, up_sum = lax.psum((logit_part, gate_part, up_part), "mp")
    chosen = jnp.take_along_axis(logits, all_ids, axis=1)
    weights = 1.0 / (1.0 + jnp.exp(chosen[:, ::-1] - chosen))
    slot_weight = (
        jnp.zeros((experts, capacity), F32)
        .at[pair_expert, position]
        .set(weights.reshape(-1))
    )
    hidden = (jax.nn.silu(gate_sum) * up_sum).astype(BF16)
    slot_out = (
        jnp.einsum("ecf,efd->ecd", hidden, w_down, preferred_element_type=F32)
        * slot_weight[:, :, None]
    )
    partial_value = (
        jnp.zeros((token_count, half_width), F32)
        .at[slot_token.reshape(-1)]
        .add(slot_out.reshape(-1, half_width), mode="drop")
    )
    mine = lax.psum_scatter(partial_value, "batch", scatter_dimension=0, tiled=True)
    return mine.astype(BF16)


def solution(mesh):
    def per_device(*args):
        rows, (experts, hidden, _) = args[0].shape[0], args[3].shape
        fits = mesh.shape["batch"] == 8 and rows % 16 == 0 and 8 * rows <= 128
        if fits and experts == 4 and hidden <= 1024:
            return fast(*args)
        return general(*args)

    in_specs = (
        P(("group", "batch"), "mp"),
        P(("group", "batch"), None),
        P("mp", None),
        P(None, "batch", "mp"),
        P(None, "batch", "mp"),
        P(None, "batch", "mp"),
    )
    out_specs = P(("group", "batch"), "mp")
    return jax.shard_map(
        per_device, mesh=mesh, in_specs=in_specs, out_specs=out_specs, check_vma=False
    )
```

```python
import functools
import jax
import jax.numpy as jnp
from jax import lax
from jax.experimental import pallas as pl
from jax.experimental.pallas import tpu as pltpu
from jax.sharding import PartitionSpec as P

F32, BF16 = jnp.float32, jnp.bfloat16
IDS = 128
SWAP = [(0, 1), (1, 0)]
HBM_BLOCK = pl.BlockSpec(memory_space=pltpu.HBM)
VMEM_BLOCK = pl.BlockSpec(memory_space=pltpu.VMEM)


def xor_send(block, mask):
    return lax.ppermute(block, "batch", [(i, i ^ mask) for i in range(8)])


def in_vmem(array):
    return pltpu.with_memory_space_constraint(array, pltpu.VMEM)


def call(kernel, outs, args, flops, size, vmem, scratch=(), hbm=()):
    specs = [HBM_BLOCK if i in hbm else VMEM_BLOCK for i in range(len(args))]
    return pl.pallas_call(
        kernel,
        out_shape=outs,
        in_specs=specs,
        out_specs=[VMEM_BLOCK] * len(outs),
        scratch_shapes=list(scratch),
        compiler_params=pltpu.CompilerParams(vmem_limit_bytes=int(vmem * 2**20)),
        cost_estimate=pl.CostEstimate(flops=flops, bytes_accessed=size, transcendentals=0),
    )(*args)


def column(row, rows):
    diagonal = lax.broadcasted_iota(jnp.int32, (rows, rows), 0) == lax.broadcasted_iota(
        jnp.int32, (rows, rows), 1
    )
    return jnp.sum(jnp.where(diagonal, row, 0.0), axis=1, keepdims=True)


def pack_kernel(tokens_ref, ids_ref, out_ref, held_ref, sems):
    rows, width = tokens_ref.shape
    copies = [
        pltpu.make_async_copy(ids_ref, held_ref, sems.at[0]),
        pltpu.make_async_copy(tokens_ref, out_ref.at[:, pl.ds(0, width)], sems.at[1]),
    ]
    for copy in copies:
        copy.start()
    copies[0].wait()
    ids = held_ref[...].astype(F32)
    lane = lax.broadcasted_iota(jnp.int32, (rows, IDS), 1)
    out_ref[:, width:] = jnp.where(
        lane == 0, column(ids[0:1], rows), column(ids[1:2], rows)
    ).astype(BF16)
    copies[1].wait()


def over_width(a, b):
    return lax.dot_general(a, b, (((1,), (1,)), ((), ())), preferred_element_type=F32)


def fetches(source_ref, experts, targets, sems, at=0):
    return [
        pltpu.make_async_copy(source_ref.at[e], target, sems.at[at + i])
        for i, (e, target) in enumerate(zip(experts, targets))
    ]


def fetch_kernel(fetched, _, source_ref, *refs):
    *held, sems = refs
    copies = fetches(source_ref, fetched, held, sems)
    for copy in copies:
        copy.start()
    for copy in copies:
        copy.wait()


def gate_kernel(fetched, *refs):
    blocks, (router_ref, w_ref, up_ref, _, x_ref, part_ref, *held, sems) = refs[:8], refs[8:]
    experts, hidden, width = w_ref.shape
    copies = fetches(up_ref, fetched, held, sems)
    for copy in copies:
        copy.start()
    rows = blocks[0].shape[0]
    for j, block in enumerate(blocks):
        x_ref[j * rows : (j + 1) * rows] = block[...]
    x = x_ref[:, :width]
    part_ref[experts * hidden :] = over_width(x, router_ref[...])
    for e in range(experts):
        part_ref[e * hidden : (e + 1) * hidden] = over_width(w_ref[e], x)
    for copy in copies:
        copy.wait()


def up_kernel(up_fetched, down_fetched, x_ref, up_ref, down_ref, *refs):
    weights, (part_ref, sent_ref, *held, sems) = refs[:2], refs[2:]
    hidden, width = weights[0].shape
    n = len(up_fetched)
    copies = fetches(up_ref, up_fetched, held[:n], sems) + fetches(
        down_ref, down_fetched, held[n:], sems, n
    )
    for copy in copies:
        copy.start()
    x = x_ref[:, :width]
    for i, w_ref in enumerate(weights):
        own = slice(i * hidden, (i + 1) * hidden)
        part = over_width(w_ref[...], x)
        part_ref[own] = part
        sent_ref[own] = part.astype(BF16)
    for copy in copies:
        copy.wait()


def factors(x_ref, gate_a, gate_b, width, base):
    count = x_ref.shape[0]
    ids = x_ref[:, width:].astype(F32)
    a, b = ids[:, 0:1], ids[:, 1:2]
    logits = gate_a[base : base + count] + gate_b[base : base + count]
    lane = lax.broadcasted_iota(jnp.int32, logits.shape, 1).astype(F32)
    is_a, is_b = lane == a, lane == b
    la = jnp.sum(jnp.where(is_a, logits, 0.0), axis=1, keepdims=True)
    lb = jnp.sum(jnp.where(is_b, logits, 0.0), axis=1, keepdims=True)
    wa = 1.0 / (1.0 + jnp.exp(lb - la))
    wb = 1.0 / (1.0 + jnp.exp(la - lb))
    return jnp.where(is_a, wa, 0.0) + jnp.where(is_b, wb, 0.0)


def hidden_units(e, i, hidden, gate_a, gate_b, up_a, up_b):
    own = slice(e * hidden, (e + 1) * hidden)
    mine = slice(i * hidden, (i + 1) * hidden)
    gate = gate_a[own] + gate_b[own]
    up = up_a[mine] + up_b[mine].astype(F32)
    return (gate / (1.0 + jnp.exp(-gate)) * up).T.astype(BF16)


def hidden_kernel(experts, fetched, gate_a, gate_b, up_a, up_b, down_ref, out_ref, *refs):
    *held, sems = refs
    copies = fetches(down_ref, fetched, held, sems)
    for copy in copies:
        copy.start()
    hidden = out_ref.shape[2]
    for i, e in enumerate(experts):
        out_ref[i] = hidden_units(e, i, hidden, gate_a, gate_b, up_a, up_b)
    for copy in copies:
        copy.wait()


def down_kernel(ready, x_ref, gate_a, gate_b, up_a, up_b, h_ref, down_ref, *refs):
    weights, outs, (held_ref, sems) = refs[:ready], refs[ready : ready + 8], refs[ready + 8 :]
    experts, hidden, width = down_ref.shape
    late = [held_ref.at[i] for i in range(experts - ready)]
    copies = fetches(down_ref, range(ready, experts), late, sems)
    for copy in copies:
        copy.start()
    half = h_ref.shape[0]
    factor = factors(x_ref, gate_a, gate_b, width, experts * hidden)
    total = None
    for e in range(experts):
        if e < half:
            h = h_ref[e]
        else:
            h = hidden_units(e, e - half, hidden, gate_a, gate_b, up_a, up_b)
        if e < ready:
            w = weights[e][...]
        else:
            copies[e - ready].wait()
            w = late[e - ready][...]
        term = factor[:, e : e + 1] * jnp.dot(h, w, preferred_element_type=F32)
        total = term if total is None else total + term
    rows = outs[0].shape[0]
    for j, out in enumerate(outs):
        out[...] = total[j * rows : (j + 1) * rows].astype(out.dtype)


def fast(tokens, expert_ids, router, w_gate, w_up, w_down):
    rows, width = tokens.shape
    experts, hidden, _ = w_gate.shape
    count, half = 8 * rows, experts // 2
    shape = lambda *s, dtype=F32: jax.ShapeDtypeStruct(s, dtype)
    in_hbm = lambda array: pltpu.with_memory_space_constraint(array, pltpu.HBM)
    (own,) = call(
        pack_kernel,
        [shape(rows, width + IDS, dtype=BF16)],
        [in_hbm(tokens), in_hbm(expert_ids.T)],
        30_000_000_000,
        4 * rows * width,
        1,
        [pltpu.VMEM(expert_ids.shape[::-1], jnp.int32), pltpu.SemaphoreType.DMA((2,))],
        hbm=(0, 1),
    )
    far = xor_send(own, 4)
    near = [xor_send(own, k) for k in (1, 2, 3)]
    forwarded = [xor_send(far, k) for k in (1, 2, 3)]
    blocks = [own, *near, far, *forwarded]

    w_gate, w_up, w_down = in_vmem(w_gate), in_hbm(w_up), in_hbm(w_down)
    flops = 2 * count * hidden * width
    size = 2 * hidden * width
    lines = jnp.pad(router.T, ((0, 128 - experts), (0, 0)))
    one = pltpu.VMEM((hidden, width), BF16)
    sems = lambda n: [pltpu.SemaphoreType.DMA((n,))]
    (up0,) = call(
        functools.partial(fetch_kernel, (0,)),
        [one],
        [far[:, :128], w_up],
        14_000_000_000,
        0,
        1,
        sems(1),
        hbm=(1,),
    )
    x, gate, up1, up2 = call(
        functools.partial(gate_kernel, (1, 2)),
        [
            shape(count, width + IDS, dtype=BF16),
            shape(experts * hidden + count, count),
            *[one] * 2,
        ],
        [*blocks, lines, w_gate, w_up, up0],
        experts * flops,
        experts * size,
        3,
        sems(2),
        hbm=(10,),
    )
    gate_other = lax.ppermute(gate, "mp", SWAP)

    def up_call(up_fetched, down_fetched, weights):
        n = len(up_fetched) + len(down_fetched)
        part, sent, *held = call(
            functools.partial(up_kernel, up_fetched, down_fetched),
            [
                shape(half * hidden, count),
                shape(half * hidden, count, dtype=BF16),
                *[one] * n,
            ],
            [x, w_up, w_down, *weights],
            half * flops,
            half * size,
            3,
            sems(n),
            hbm=(1, 2),
        )
        return (part, lax.ppermute(sent, "mp", SWAP)), held

    first, (up3,) = up_call((3,), (), (up0, up1))
    second, (down0, down1) = up_call((), (0, 1), (up2, up3))
    units, down2 = call(
        functools.partial(hidden_kernel, range(half), (2,)),
        [shape(half, count, hidden, dtype=BF16), one],
        [gate, gate_other, *first, w_down],
        0,
        12 * half * hidden * count,
        4,
        sems(1),
        hbm=(4,),
    )
    parts = call(
        functools.partial(down_kernel, 3),
        [shape(rows, width)] + [shape(rows, width, dtype=BF16)] * 7,
        [x, gate, gate_other, *second, units, w_down, down0, down1, down2],
        experts * flops,
        experts * size,
        10,
        [pltpu.VMEM((1, hidden, width), BF16), *sems(1)],
        hbm=(6,),
    )
    far_sums = [xor_send(parts[4 ^ k], k) for k in (3, 2, 1)]
    near_sums = [xor_send(parts[k], k) for k in (3, 2, 1)]
    add = lambda arrays: sum(a.astype(F32) for a in arrays)
    crossing = xor_send(add([parts[4], *far_sums]).astype(BF16), 4)
    return add([parts[0], *near_sums, crossing]).astype(BF16)


def general(tokens, expert_ids, router, w_gate, w_up, w_down):
    gathered, all_ids = (
        lax.all_gather(tokens, "batch", axis=0, tiled=True),
        lax.all_gather(expert_ids, "batch", axis=0, tiled=True),
    )
    token_count = gathered.shape[0]
    half_width = gathered.shape[1]
    experts = w_gate.shape[0]
    capacity = 3 * token_count // 4
    pair_expert = all_ids.reshape(-1)
    onehot = (pair_expert[:, None] == jnp.arange(experts, dtype=jnp.int32)[None, :]).astype(
        jnp.int32
    )
    position = jnp.sum((jnp.cumsum(onehot, axis=0) - 1) * onehot, axis=1)
    pair_token = jnp.arange(2 * token_count, dtype=jnp.int32) // 2
    slot_token = (
        jnp.full((experts, capacity), token_count, jnp.int32)
        .at[pair_expert, position]
        .set(pair_token)
    )
    slot_rows = jnp.take(gathered, jnp.minimum(slot_token, token_count - 1), axis=0)
    logit_part = jnp.dot(gathered, router, preferred_element_type=F32)
    gate_part = jnp.einsum("ecd,efd->ecf", slot_rows, w_gate, preferred_element_type=F32)
    up_part = jnp.einsum("ecd,efd->ecf", slot_rows, w_up, preferred_element_type=F32)
    logits, gate_sum, up_sum = lax.psum((logit_part, gate_part, up_part), "mp")
    chosen = jnp.take_along_axis(logits, all_ids, axis=1)
    weights = 1.0 / (1.0 + jnp.exp(chosen[:, ::-1] - chosen))
    slot_weight = (
        jnp.zeros((experts, capacity), F32)
        .at[pair_expert, position]
        .set(weights.reshape(-1))
    )
    hidden = (jax.nn.silu(gate_sum) * up_sum).astype(BF16)
    slot_out = (
        jnp.einsum("ecf,efd->ecd", hidden, w_down, preferred_element_type=F32)
        * slot_weight[:, :, None]
    )
    partial_value = (
        jnp.zeros((token_count, half_width), F32)
        .at[slot_token.reshape(-1)]
        .add(slot_out.reshape(-1, half_width), mode="drop")
    )
    mine = lax.psum_scatter(partial_value, "batch", scatter_dimension=0, tiled=True)
    return mine.astype(BF16)


def solution(mesh):
    def per_device(*args):
        rows, (experts, hidden, _) = args[0].shape[0], args[3].shape
        fits = mesh.shape["batch"] == 8 and rows % 16 == 0 and 8 * rows <= 128
        if fits and experts == 4 and hidden <= 1024:
            return fast(*args)
        return general(*args)

    in_specs = (
        P(("group", "batch"), "mp"),
        P(("group", "batch"), None),
        P("mp", None),
        P(None, "batch", "mp"),
        P(None, "batch", "mp"),
        P(None, "batch", "mp"),
    )
    out_specs = P(("group", "batch"), "mp")
    return jax.shard_map(
        per_device, mesh=mesh, in_specs=in_specs, out_specs=out_specs, check_vma=False
    )
```

```python
import functools
import jax
import jax.numpy as jnp
from jax import lax
from jax.experimental import pallas as pl
from jax.experimental.pallas import tpu as pltpu
from jax.sharding import PartitionSpec as P

F32, BF16 = jnp.float32, jnp.bfloat16
IDS = 128
SWAP = [(0, 1), (1, 0)]
HBM_BLOCK = pl.BlockSpec(memory_space=pltpu.HBM)
VMEM_BLOCK = pl.BlockSpec(memory_space=pltpu.VMEM)


def xor_send(block, mask):
    return lax.ppermute(block, "batch", [(i, i ^ mask) for i in range(8)])


def in_vmem(array):
    return pltpu.with_memory_space_constraint(array, pltpu.VMEM)


def call(kernel, outs, args, flops, size, vmem, scratch=(), hbm=()):
    specs = [HBM_BLOCK if i in hbm else VMEM_BLOCK for i in range(len(args))]
    return pl.pallas_call(
        kernel,
        out_shape=outs,
        in_specs=specs,
        out_specs=[VMEM_BLOCK] * len(outs),
        scratch_shapes=list(scratch),
        compiler_params=pltpu.CompilerParams(vmem_limit_bytes=int(vmem * 2**20)),
        cost_estimate=pl.CostEstimate(flops=flops, bytes_accessed=size, transcendentals=0),
    )(*args)


def column(row, rows):
    diagonal = lax.broadcasted_iota(jnp.int32, (rows, rows), 0) == lax.broadcasted_iota(
        jnp.int32, (rows, rows), 1
    )
    return jnp.sum(jnp.where(diagonal, row, 0.0), axis=1, keepdims=True)


def pack_kernel(tokens_ref, ids_ref, out_ref, held_ref, sems):
    rows, width = tokens_ref.shape
    copies = [
        pltpu.make_async_copy(ids_ref, held_ref, sems.at[0]),
        pltpu.make_async_copy(tokens_ref, out_ref.at[:, pl.ds(0, width)], sems.at[1]),
    ]
    for copy in copies:
        copy.start()
    copies[0].wait()
    ids = held_ref[...].astype(F32)
    lane = lax.broadcasted_iota(jnp.int32, (rows, IDS), 1)
    out_ref[:, width:] = jnp.where(
        lane == 0, column(ids[0:1], rows), column(ids[1:2], rows)
    ).astype(BF16)
    copies[1].wait()


def over_width(a, b):
    return lax.dot_general(a, b, (((1,), (1,)), ((), ())), preferred_element_type=F32)


def fetches(source_ref, units, targets, sems, at=0):
    rows, copies = targets[0].shape[0] if targets else 0, []
    for i, (unit, target) in enumerate(zip(units, targets)):
        per_expert = source_ref.shape[1] // rows
        source = source_ref.at[unit // per_expert, pl.ds(unit % per_expert * rows, rows)]
        copies.append(pltpu.make_async_copy(source, target, sems.at[at + i]))
    return copies


def fetch_kernel(fetched, _, source_ref, *refs):
    *held, sems = refs
    copies = fetches(source_ref, fetched, held, sems)
    for copy in copies:
        copy.start()
    for copy in copies:
        copy.wait()


def gate_kernel(fetched, carried, *refs):
    blocks, (router_ref, w_ref, up_ref), refs = refs[:8], refs[8:11], refs[11 + carried :]
    x_ref, part_ref, *held, sems = refs
    experts, hidden, width = w_ref.shape
    copies = fetches(up_ref, fetched, held, sems)
    for copy in copies:
        copy.start()
    rows = blocks[0].shape[0]
    for j, block in enumerate(blocks):
        x_ref[j * rows : (j + 1) * rows] = block[...]
    x = x_ref[:, :width]
    part_ref[experts * hidden :] = over_width(x, router_ref[...])
    for e in range(experts):
        part_ref[e * hidden : (e + 1) * hidden] = over_width(w_ref[e], x)
    for copy in copies:
        copy.wait()


def up_kernel(ready, carried, up_fetched, down_fetched, x_ref, up_ref, down_ref, *refs):
    weights, (part_ref, sent_ref, *held, sems) = refs[:ready], refs[ready + carried :]
    rows, width = weights[0].shape
    n = len(up_fetched)
    copies = fetches(up_ref, up_fetched, held[:n], sems) + fetches(
        down_ref, down_fetched, held[n:], sems, n
    )
    for copy in copies:
        copy.start()
    x = x_ref[:, :width]
    for i, w_ref in enumerate(weights):
        own = slice(i * rows, (i + 1) * rows)
        part = over_width(w_ref[...], x)
        part_ref[own] = part
        sent_ref[own] = part.astype(BF16)
    for copy in copies:
        copy.wait()


def factors(x_ref, gate_a, gate_b, width, base):
    count = x_ref.shape[0]
    ids = x_ref[:, width:].astype(F32)
    a, b = ids[:, 0:1], ids[:, 1:2]
    logits = gate_a[base : base + count] + gate_b[base : base + count]
    lane = lax.broadcasted_iota(jnp.int32, logits.shape, 1).astype(F32)
    is_a, is_b = lane == a, lane == b
    la = jnp.sum(jnp.where(is_a, logits, 0.0), axis=1, keepdims=True)
    lb = jnp.sum(jnp.where(is_b, logits, 0.0), axis=1, keepdims=True)
    wa = 1.0 / (1.0 + jnp.exp(lb - la))
    wb = 1.0 / (1.0 + jnp.exp(la - lb))
    return jnp.where(is_a, wa, 0.0) + jnp.where(is_b, wb, 0.0)


def hidden_units(e, i, hidden, gate_a, gate_b, up_a, up_b):
    own = slice(e * hidden, (e + 1) * hidden)
    mine = slice(i * hidden, (i + 1) * hidden)
    gate = gate_a[own] + gate_b[own]
    up = up_a[mine] + up_b[mine].astype(F32)
    return (gate / (1.0 + jnp.exp(-gate)) * up).T.astype(BF16)


def hidden_kernel(experts, fetched, carried, gate_a, gate_b, up_a, up_b, down_ref, *refs):
    out_ref, *held, sems = refs[carried:]
    copies = fetches(down_ref, fetched, held, sems)
    for copy in copies:
        copy.start()
    hidden = out_ref.shape[2]
    for i, e in enumerate(experts):
        out_ref[i] = hidden_units(e, i, hidden, gate_a, gate_b, up_a, up_b)
    for copy in copies:
        copy.wait()


def down_kernel(ready, x_ref, gate_a, gate_b, up_a, up_b, h_ref, down_ref, *refs):
    weights, outs, (held_ref, sems) = refs[:ready], refs[ready : ready + 8], refs[ready + 8 :]
    experts, hidden, width = down_ref.shape
    late, tile = held_ref.shape[:2]
    weights = list(weights) + [held_ref.at[i] for i in range(late)]
    copies = fetches(down_ref, range(ready, ready + late), weights[ready:], sems)
    for copy in copies:
        copy.start()
    half, per_expert = h_ref.shape[0], hidden // tile
    factor = factors(x_ref, gate_a, gate_b, width, experts * hidden)
    total = None
    for e in range(experts):
        if e < half:
            h = h_ref[e]
        else:
            h = hidden_units(e, e - half, hidden, gate_a, gate_b, up_a, up_b)
        term = None
        for i in range(per_expert):
            unit = e * per_expert + i
            if unit >= ready:
                copies[unit - ready].wait()
            dot = jnp.dot(
                h[:, i * tile : (i + 1) * tile], weights[unit][...], preferred_element_type=F32
            )
            term = dot if term is None else term + dot
        term = factor[:, e : e + 1] * term
        total = term if total is None else total + term
    rows = outs[0].shape[0]
    for j, out in enumerate(outs):
        out[...] = total[j * rows : (j + 1) * rows].astype(out.dtype)


def fast(tokens, expert_ids, router, w_gate, w_up, w_down):
    rows, width = tokens.shape
    experts, hidden, _ = w_gate.shape
    count, half = 8 * rows, experts // 2
    shape = lambda *s, dtype=F32: jax.ShapeDtypeStruct(s, dtype)
    in_hbm = lambda array: pltpu.with_memory_space_constraint(array, pltpu.HBM)
    (own,) = call(
        pack_kernel,
        [shape(rows, width + IDS, dtype=BF16)],
        [in_hbm(tokens), in_hbm(expert_ids.T)],
        30_000_000_000,
        4 * rows * width,
        1,
        [pltpu.VMEM(expert_ids.shape[::-1], jnp.int32), pltpu.SemaphoreType.DMA((2,))],
        hbm=(0, 1),
    )
    far = xor_send(own, 4)
    near = [xor_send(own, k) for k in (1, 2, 3)]
    forwarded = [xor_send(far, k) for k in (1, 2, 3)]
    blocks = [own, *near, far, *forwarded]

    w_gate, w_up, w_down = in_vmem(w_gate), in_hbm(w_up), in_hbm(w_down)
    flops = 2 * count * hidden * width
    size = 2 * hidden * width
    lines = jnp.pad(router.T, ((0, 128 - experts), (0, 0)))
    tile = hidden // 2
    one = pltpu.VMEM((tile, width), BF16)
    sems = lambda n: [pltpu.SemaphoreType.DMA((n,))]
    up_early, up_next, up_last = (0, 1, 2), (3, 4, 5, 6), (7,)
    down_first, down_second, down_third, late = (0, 1), (2, 3, 4), (5,), 2
    early = call(
        functools.partial(fetch_kernel, up_early),
        [one] * len(up_early),
        [far[:, :128], w_up],
        8_000_000_000,
        0,
        1,
        sems(len(up_early)),
        hbm=(1,),
    )
    x, gate, *following = call(
        functools.partial(gate_kernel, up_next, len(up_early)),
        [
            shape(count, width + IDS, dtype=BF16),
            shape(experts * hidden + count, count),
            *[one] * len(up_next),
        ],
        [*blocks, lines, w_gate, w_up, *early],
        experts * flops,
        experts * size,
        3,
        sems(len(up_next)),
        hbm=(10,),
    )
    gate_other = lax.ppermute(gate, "mp", SWAP)

    def up_call(up_fetched, down_fetched, weights, carried):
        n = len(up_fetched) + len(down_fetched)
        part, sent, *held = call(
            functools.partial(up_kernel, len(weights), len(carried), up_fetched, down_fetched),
            [
                shape(half * hidden, count),
                shape(half * hidden, count, dtype=BF16),
                *[one] * n,
            ],
            [x, w_up, w_down, *weights, *carried],
            half * flops,
            half * size,
            3,
            sems(n),
            hbm=(1, 2),
        )
        return (part, lax.ppermute(sent, "mp", SWAP)), held

    units = [*early, *following]
    first, held = up_call(up_last, down_first, units[:experts], units[experts:])
    units += held[: len(up_last)]
    downs = held[len(up_last) :]
    second, held = up_call((), down_second, units[experts:], downs)
    downs += held
    h, *held = call(
        functools.partial(hidden_kernel, range(half), down_third, len(downs)),
        [shape(half, count, hidden, dtype=BF16)] + [one] * len(down_third),
        [gate, gate_other, *first, w_down, *downs],
        0,
        12 * half * hidden * count,
        4,
        sems(len(down_third)),
        hbm=(4,),
    )
    downs += held
    parts = call(
        functools.partial(down_kernel, len(downs)),
        [shape(rows, width)] + [shape(rows, width, dtype=BF16)] * 7,
        [x, gate, gate_other, *second, h, w_down, *downs],
        experts * flops,
        experts * size,
        16,
        [pltpu.VMEM((late, tile, width), BF16), *sems(late)],
        hbm=(6,),
    )
    far_sums = [xor_send(parts[4 ^ k], k) for k in (3, 2, 1)]
    near_sums = [xor_send(parts[k], k) for k in (3, 2, 1)]
    add = lambda arrays: sum(a.astype(F32) for a in arrays)
    crossing = xor_send(add([parts[4], *far_sums]).astype(BF16), 4)
    return add([parts[0], *near_sums, crossing]).astype(BF16)


def general(tokens, expert_ids, router, w_gate, w_up, w_down):
    gathered, all_ids = (
        lax.all_gather(tokens, "batch", axis=0, tiled=True),
        lax.all_gather(expert_ids, "batch", axis=0, tiled=True),
    )
    token_count = gathered.shape[0]
    half_width = gathered.shape[1]
    experts = w_gate.shape[0]
    capacity = 3 * token_count // 4
    pair_expert = all_ids.reshape(-1)
    onehot = (pair_expert[:, None] == jnp.arange(experts, dtype=jnp.int32)[None, :]).astype(
        jnp.int32
    )
    position = jnp.sum((jnp.cumsum(onehot, axis=0) - 1) * onehot, axis=1)
    pair_token = jnp.arange(2 * token_count, dtype=jnp.int32) // 2
    slot_token = (
        jnp.full((experts, capacity), token_count, jnp.int32)
        .at[pair_expert, position]
        .set(pair_token)
    )
    slot_rows = jnp.take(gathered, jnp.minimum(slot_token, token_count - 1), axis=0)
    logit_part = jnp.dot(gathered, router, preferred_element_type=F32)
    gate_part = jnp.einsum("ecd,efd->ecf", slot_rows, w_gate, preferred_element_type=F32)
    up_part = jnp.einsum("ecd,efd->ecf", slot_rows, w_up, preferred_element_type=F32)
    logits, gate_sum, up_sum = lax.psum((logit_part, gate_part, up_part), "mp")
    chosen = jnp.take_along_axis(logits, all_ids, axis=1)
    weights = 1.0 / (1.0 + jnp.exp(chosen[:, ::-1] - chosen))
    slot_weight = (
        jnp.zeros((experts, capacity), F32)
        .at[pair_expert, position]
        .set(weights.reshape(-1))
    )
    hidden = (jax.nn.silu(gate_sum) * up_sum).astype(BF16)
    slot_out = (
        jnp.einsum("ecf,efd->ecd", hidden, w_down, preferred_element_type=F32)
        * slot_weight[:, :, None]
    )
    partial_value = (
        jnp.zeros((token_count, half_width), F32)
        .at[slot_token.reshape(-1)]
        .add(slot_out.reshape(-1, half_width), mode="drop")
    )
    mine = lax.psum_scatter(partial_value, "batch", scatter_dimension=0, tiled=True)
    return mine.astype(BF16)


def solution(mesh):
    def per_device(*args):
        rows, (experts, hidden, _) = args[0].shape[0], args[3].shape
        fits = mesh.shape["batch"] == 8 and rows % 16 == 0 and 8 * rows <= 128
        if fits and experts == 4 and hidden <= 1024:
            return fast(*args)
        return general(*args)

    in_specs = (
        P(("group", "batch"), "mp"),
        P(("group", "batch"), None),
        P("mp", None),
        P(None, "batch", "mp"),
        P(None, "batch", "mp"),
        P(None, "batch", "mp"),
    )
    out_specs = P(("group", "batch"), "mp")
    return jax.shard_map(
        per_device, mesh=mesh, in_specs=in_specs, out_specs=out_specs, check_vma=False
    )
```

```python
import functools
import jax
import jax.numpy as jnp
from jax import lax
from jax.experimental import pallas as pl
from jax.experimental.pallas import tpu as pltpu
from jax.sharding import PartitionSpec as P

F32, BF16 = jnp.float32, jnp.bfloat16
IDS = 128
SWAP = [(0, 1), (1, 0)]
HBM_BLOCK = pl.BlockSpec(memory_space=pltpu.HBM)
VMEM_BLOCK = pl.BlockSpec(memory_space=pltpu.VMEM)


def xor_send(block, mask):
    return lax.ppermute(block, "batch", [(i, i ^ mask) for i in range(8)])


def in_vmem(array):
    return pltpu.with_memory_space_constraint(array, pltpu.VMEM)


def call(kernel, outs, args, flops, size, vmem, scratch=(), hbm=()):
    specs = [HBM_BLOCK if i in hbm else VMEM_BLOCK for i in range(len(args))]
    return pl.pallas_call(
        kernel,
        out_shape=outs,
        in_specs=specs,
        out_specs=[VMEM_BLOCK] * len(outs),
        scratch_shapes=list(scratch),
        compiler_params=pltpu.CompilerParams(vmem_limit_bytes=int(vmem * 2**20)),
        cost_estimate=pl.CostEstimate(flops=flops, bytes_accessed=size, transcendentals=0),
    )(*args)


def column(row, rows):
    diagonal = lax.broadcasted_iota(jnp.int32, (rows, rows), 0) == lax.broadcasted_iota(
        jnp.int32, (rows, rows), 1
    )
    return jnp.sum(jnp.where(diagonal, row, 0.0), axis=1, keepdims=True)


def pack_kernel(tokens_ref, ids_ref, out_ref, held_ref, sems):
    rows, width = tokens_ref.shape
    copies = [
        pltpu.make_async_copy(ids_ref, held_ref, sems.at[0]),
        pltpu.make_async_copy(tokens_ref, out_ref.at[:, pl.ds(0, width)], sems.at[1]),
    ]
    for copy in copies:
        copy.start()
    copies[0].wait()
    ids = held_ref[...].astype(F32)
    lane = lax.broadcasted_iota(jnp.int32, (rows, IDS), 1)
    out_ref[:, width:] = jnp.where(
        lane == 0, column(ids[0:1], rows), column(ids[1:2], rows)
    ).astype(BF16)
    copies[1].wait()


def over_width(a, b):
    return lax.dot_general(a, b, (((1,), (1,)), ((), ())), preferred_element_type=F32)


def fetches(source_ref, wanted, targets, sems, at=0):
    copies = []
    for i, (place, target) in enumerate(zip(wanted, targets)):
        rows = target.shape[0]
        e, first = place if isinstance(place, tuple) else (place, 0)
        copies.append(
            pltpu.make_async_copy(
                source_ref.at[e, pl.ds(first, rows)], target, sems.at[at + i]
            )
        )
    return copies


def fetch_kernel(fetched, _, source_ref, *refs):
    *held, sems = refs
    copies = fetches(source_ref, fetched, held, sems)
    for copy in copies:
        copy.start()
    for copy in copies:
        copy.wait()


def gate_kernel(fetched, carried, *refs):
    blocks, (router_ref, w_ref, up_ref), refs = refs[:8], refs[8:11], refs[11 + carried :]
    x_ref, part_ref, *held, sems = refs
    experts, hidden, width = w_ref.shape
    copies = fetches(up_ref, fetched, held, sems)
    for copy in copies:
        copy.start()
    rows = blocks[0].shape[0]
    for j, block in enumerate(blocks):
        x_ref[j * rows : (j + 1) * rows] = block[...]
    x = x_ref[:, :width]
    part_ref[experts * hidden :] = over_width(x, router_ref[...])
    for e in range(experts):
        part_ref[e * hidden : (e + 1) * hidden] = over_width(w_ref[e], x)
    for copy in copies:
        copy.wait()


def up_kernel(ready, carried, up_fetched, down_fetched, x_ref, up_ref, down_ref, *refs):
    weights, (part_ref, sent_ref, *held, sems) = refs[:ready], refs[ready + carried :]
    width = weights[0].shape[1]
    n = len(up_fetched)
    copies = fetches(up_ref, up_fetched, held[:n], sems) + fetches(
        down_ref, down_fetched, held[n:], sems, n
    )
    for copy in copies:
        copy.start()
    x, at = x_ref[:, :width], 0
    for w_ref in weights:
        own = slice(at, at + w_ref.shape[0])
        part = over_width(w_ref[...], x)
        part_ref[own] = part
        sent_ref[own] = part.astype(BF16)
        at += w_ref.shape[0]
    for copy in copies:
        copy.wait()


def factors(x_ref, gate_a, gate_b, width, base):
    count = x_ref.shape[0]
    ids = x_ref[:, width:].astype(F32)
    a, b = ids[:, 0:1], ids[:, 1:2]
    logits = gate_a[base : base + count] + gate_b[base : base + count]
    lane = lax.broadcasted_iota(jnp.int32, logits.shape, 1).astype(F32)
    is_a, is_b = lane == a, lane == b
    la = jnp.sum(jnp.where(is_a, logits, 0.0), axis=1, keepdims=True)
    lb = jnp.sum(jnp.where(is_b, logits, 0.0), axis=1, keepdims=True)
    wa = 1.0 / (1.0 + jnp.exp(lb - la))
    wb = 1.0 / (1.0 + jnp.exp(la - lb))
    return jnp.where(is_a, wa, 0.0) + jnp.where(is_b, wb, 0.0)


def hidden_units(e, i, hidden, gate_a, gate_b, up_a, up_b):
    own = slice(e * hidden, (e + 1) * hidden)
    mine = slice(i * hidden, (i + 1) * hidden)
    gate = gate_a[own] + gate_b[own]
    up = up_a[mine] + up_b[mine].astype(F32)
    return (gate / (1.0 + jnp.exp(-gate)) * up).T.astype(BF16)


def hidden_kernel(experts, fetched, gate_a, gate_b, up_a, up_b, down_ref, *refs):
    out_ref, *held, sems = refs[2:]
    copies = fetches(down_ref, fetched, held, sems)
    for copy in copies:
        copy.start()
    hidden = out_ref.shape[2]
    for i, e in enumerate(experts):
        out_ref[i] = hidden_units(e, i, hidden, gate_a, gate_b, up_a, up_b)
    for copy in copies:
        copy.wait()


def down_kernel(ready, x_ref, gate_a, gate_b, up_a, up_b, h_ref, down_ref, *refs):
    weights, outs, (held_ref, sems) = refs[:ready], refs[ready : ready + 8], refs[ready + 8 :]
    experts, hidden, width = down_ref.shape
    late = [held_ref.at[i] for i in range(experts - ready)]
    copies = fetches(down_ref, range(ready, experts), late, sems)
    for copy in copies:
        copy.start()
    half = h_ref.shape[0]
    factor = factors(x_ref, gate_a, gate_b, width, experts * hidden)
    total = None
    for e in range(experts):
        if e < half:
            h = h_ref[e]
        else:
            h = hidden_units(e, e - half, hidden, gate_a, gate_b, up_a, up_b)
        if e < ready:
            w = weights[e][...]
        else:
            copies[e - ready].wait()
            w = late[e - ready][...]
        term = factor[:, e : e + 1] * jnp.dot(h, w, preferred_element_type=F32)
        total = term if total is None else total + term
    rows = outs[0].shape[0]
    for j, out in enumerate(outs):
        out[...] = total[j * rows : (j + 1) * rows].astype(out.dtype)


def fast(tokens, expert_ids, router, w_gate, w_up, w_down):
    rows, width = tokens.shape
    experts, hidden, _ = w_gate.shape
    count, half = 8 * rows, experts // 2
    shape = lambda *s, dtype=F32: jax.ShapeDtypeStruct(s, dtype)
    in_hbm = lambda array: pltpu.with_memory_space_constraint(array, pltpu.HBM)
    (own,) = call(
        pack_kernel,
        [shape(rows, width + IDS, dtype=BF16)],
        [in_hbm(tokens), in_hbm(expert_ids.T)],
        30_000_000_000,
        4 * rows * width,
        1,
        [pltpu.VMEM(expert_ids.shape[::-1], jnp.int32), pltpu.SemaphoreType.DMA((2,))],
        hbm=(0, 1),
    )
    far = xor_send(own, 4)
    near = [xor_send(own, k) for k in (3, 2, 1)]
    forwarded = [xor_send(far, k) for k in (3, 2, 1)]
    blocks = [own, *near[::-1], far, *forwarded[::-1]]

    w_gate, w_up, w_down = in_vmem(w_gate), in_hbm(w_up), in_hbm(w_down)
    flops = 2 * count * hidden * width
    size = 2 * hidden * width
    lines = jnp.pad(router.T, ((0, 128 - experts), (0, 0)))
    one = pltpu.VMEM((hidden, width), BF16)
    part_of_one = pltpu.VMEM((hidden // 2, width), BF16)
    sems = lambda n: [pltpu.SemaphoreType.DMA((n,))]
    (up0,) = call(
        functools.partial(fetch_kernel, (0,)),
        [one] * 1,
        [far[:, :128], w_up],
        14_000_000_000,
        0,
        1,
        sems(1),
        hbm=(1,),
    )
    x, gate, up1, up2, up3a = call(
        functools.partial(gate_kernel, (1, 2, (3, 0)), 1),
        [
            shape(count, width + IDS, dtype=BF16),
            shape(experts * hidden + count, count),
            *[one] * 2,
            part_of_one,
        ],
        [*blocks, lines, w_gate, w_up, up0],
        experts * flops,
        experts * size,
        3,
        sems(3),
        hbm=(10,),
    )
    gate_other = lax.ppermute(gate, "mp", SWAP)

    def up_call(up_fetched, down_fetched, weights, held, carried):
        n = len(held)
        part, sent, *held = call(
            functools.partial(up_kernel, len(weights), len(carried), up_fetched, down_fetched),
            [
                shape(half * hidden, count),
                shape(half * hidden, count, dtype=BF16),
                *held,
            ],
            [x, w_up, w_down, *weights, *carried],
            half * flops,
            half * size,
            3,
            sems(max(n, 1)),
            hbm=(1, 2),
        )
        return (part, lax.ppermute(sent, "mp", SWAP)), held

    first, (up3b, down0) = up_call(
        ((3, hidden // 2),), (0,), (up0, up1), (part_of_one, one), (up3a,)
    )
    second, (down1,) = up_call((), (1,), (up2, up3a, up3b), (one,), ())
    units, down2 = call(
        functools.partial(hidden_kernel, range(half), (2,)),
        [shape(half, count, hidden, dtype=BF16)] + [one] * 1,
        [gate, gate_other, *first, w_down, down0, down1],
        0,
        12 * half * hidden * count,
        4,
        sems(1),
        hbm=(4,),
    )
    parts = call(
        functools.partial(down_kernel, 3),
        [shape(rows, width)] + [shape(rows, width, dtype=BF16)] * 7,
        [x, gate, gate_other, *second, units, w_down, down0, down1, down2],
        experts * flops,
        experts * size,
        10,
        [pltpu.VMEM((1, hidden, width), BF16), *sems(1)],
        hbm=(6,),
    )
    far_sums = [xor_send(parts[4 ^ k], k) for k in (3, 2, 1)]
    near_sums = [xor_send(parts[k], k) for k in (3, 2, 1)]
    add = lambda arrays: sum(a.astype(F32) for a in arrays)
    crossing = xor_send(add([parts[4], *far_sums]).astype(BF16), 4)
    return add([parts[0], *near_sums, crossing]).astype(BF16)


def general(tokens, expert_ids, router, w_gate, w_up, w_down):
    gathered, all_ids = (
        lax.all_gather(tokens, "batch", axis=0, tiled=True),
        lax.all_gather(expert_ids, "batch", axis=0, tiled=True),
    )
    token_count = gathered.shape[0]
    half_width = gathered.shape[1]
    experts = w_gate.shape[0]
    capacity = 3 * token_count // 4
    pair_expert = all_ids.reshape(-1)
    onehot = (pair_expert[:, None] == jnp.arange(experts, dtype=jnp.int32)[None, :]).astype(
        jnp.int32
    )
    position = jnp.sum((jnp.cumsum(onehot, axis=0) - 1) * onehot, axis=1)
    pair_token = jnp.arange(2 * token_count, dtype=jnp.int32) // 2
    slot_token = (
        jnp.full((experts, capacity), token_count, jnp.int32)
        .at[pair_expert, position]
        .set(pair_token)
    )
    slot_rows = jnp.take(gathered, jnp.minimum(slot_token, token_count - 1), axis=0)
    logit_part = jnp.dot(gathered, router, preferred_element_type=F32)
    gate_part = jnp.einsum("ecd,efd->ecf", slot_rows, w_gate, preferred_element_type=F32)
    up_part = jnp.einsum("ecd,efd->ecf", slot_rows, w_up, preferred_element_type=F32)
    logits, gate_sum, up_sum = lax.psum((logit_part, gate_part, up_part), "mp")
    chosen = jnp.take_along_axis(logits, all_ids, axis=1)
    weights = 1.0 / (1.0 + jnp.exp(chosen[:, ::-1] - chosen))
    slot_weight = (
        jnp.zeros((experts, capacity), F32)
        .at[pair_expert, position]
        .set(weights.reshape(-1))
    )
    hidden = (jax.nn.silu(gate_sum) * up_sum).astype(BF16)
    slot_out = (
        jnp.einsum("ecf,efd->ecd", hidden, w_down, preferred_element_type=F32)
        * slot_weight[:, :, None]
    )
    partial_value = (
        jnp.zeros((token_count, half_width), F32)
        .at[slot_token.reshape(-1)]
        .add(slot_out.reshape(-1, half_width), mode="drop")
    )
    mine = lax.psum_scatter(partial_value, "batch", scatter_dimension=0, tiled=True)
    return mine.astype(BF16)


def solution(mesh):
    def per_device(*args):
        rows, (experts, hidden, _) = args[0].shape[0], args[3].shape
        fits = mesh.shape["batch"] == 8 and rows % 16 == 0 and 8 * rows <= 128
        if fits and experts == 4 and hidden <= 1024:
            return fast(*args)
        return general(*args)

    in_specs = (
        P(("group", "batch"), "mp"),
        P(("group", "batch"), None),
        P("mp", None),
        P(None, "batch", "mp"),
        P(None, "batch", "mp"),
        P(None, "batch", "mp"),
    )
    out_specs = P(("group", "batch"), "mp")
    return jax.shard_map(
        per_device, mesh=mesh, in_specs=in_specs, out_specs=out_specs, check_vma=False
    )
```

```python
import functools
import jax
import jax.numpy as jnp
from jax import lax
from jax.experimental import pallas as pl
from jax.experimental.pallas import tpu as pltpu
from jax.sharding import PartitionSpec as P

F32, BF16 = jnp.float32, jnp.bfloat16
IDS = 128
SWAP = [(0, 1), (1, 0)]
HBM_BLOCK = pl.BlockSpec(memory_space=pltpu.HBM)
VMEM_BLOCK = pl.BlockSpec(memory_space=pltpu.VMEM)


def xor_send(block, mask):
    return lax.ppermute(block, "batch", [(i, i ^ mask) for i in range(8)])


def in_vmem(array):
    return pltpu.with_memory_space_constraint(array, pltpu.VMEM)


def call(kernel, outs, args, flops, size, vmem, scratch=(), hbm=()):
    specs = [HBM_BLOCK if i in hbm else VMEM_BLOCK for i in range(len(args))]
    return pl.pallas_call(
        kernel,
        out_shape=outs,
        in_specs=specs,
        out_specs=[VMEM_BLOCK] * len(outs),
        scratch_shapes=list(scratch),
        compiler_params=pltpu.CompilerParams(vmem_limit_bytes=int(vmem * 2**20)),
        cost_estimate=pl.CostEstimate(flops=flops, bytes_accessed=size, transcendentals=0),
    )(*args)


def column(row, rows):
    diagonal = lax.broadcasted_iota(jnp.int32, (rows, rows), 0) == lax.broadcasted_iota(
        jnp.int32, (rows, rows), 1
    )
    return jnp.sum(jnp.where(diagonal, row, 0.0), axis=1, keepdims=True)


def pack_kernel(tokens_ref, ids_ref, out_ref, held_ref, sems):
    rows, width = tokens_ref.shape
    copies = [
        pltpu.make_async_copy(ids_ref, held_ref, sems.at[0]),
        pltpu.make_async_copy(tokens_ref, out_ref.at[:, pl.ds(0, width)], sems.at[1]),
    ]
    for copy in copies:
        copy.start()
    copies[0].wait()
    ids = held_ref[...].astype(F32)
    lane = lax.broadcasted_iota(jnp.int32, (rows, IDS), 1)
    out_ref[:, width:] = jnp.where(
        lane == 0, column(ids[0:1], rows), column(ids[1:2], rows)
    ).astype(BF16)
    copies[1].wait()


def over_width(a, b):
    return lax.dot_general(a, b, (((1,), (1,)), ((), ())), preferred_element_type=F32)


def fetches(source_ref, wanted, targets, sems, at=0):
    copies = []
    for i, (place, target) in enumerate(zip(wanted, targets)):
        rows = target.shape[0]
        e, first = place if isinstance(place, tuple) else (place, 0)
        copies.append(
            pltpu.make_async_copy(
                source_ref.at[e, pl.ds(first, rows)], target, sems.at[at + i]
            )
        )
    return copies


def fetch_kernel(fetched, _, source_ref, *refs):
    *held, sems = refs
    copies = fetches(source_ref, fetched, held, sems)
    for copy in copies:
        copy.start()
    for copy in copies:
        copy.wait()


def gate_kernel(fetched, carried, *refs):
    blocks, (router_ref, w_ref, up_ref), refs = refs[:8], refs[8:11], refs[11 + carried :]
    x_ref, part_ref, *held, sems = refs
    experts, hidden, width = w_ref.shape
    copies = fetches(up_ref, fetched, held, sems)
    for copy in copies:
        copy.start()
    rows = blocks[0].shape[0]
    for j, block in enumerate(blocks):
        x_ref[j * rows : (j + 1) * rows] = block[...]
    x = x_ref[:, :width]
    part_ref[experts * hidden :] = over_width(x, router_ref[...])
    for e in range(experts):
        part_ref[e * hidden : (e + 1) * hidden] = over_width(w_ref[e], x)
    for copy in copies:
        copy.wait()


def up_kernel(ready, carried, up_fetched, down_fetched, x_ref, up_ref, down_ref, *refs):
    weights, (part_ref, sent_ref, *held, sems) = refs[:ready], refs[ready + carried :]
    width = weights[0].shape[1]
    n = len(up_fetched)
    copies = fetches(up_ref, up_fetched, held[:n], sems) + fetches(
        down_ref, down_fetched, held[n:], sems, n
    )
    for copy in copies:
        copy.start()
    x, at = x_ref[:, :width], 0
    for w_ref in weights:
        own = slice(at, at + w_ref.shape[0])
        part = over_width(w_ref[...], x)
        part_ref[own] = part
        sent_ref[own] = part.astype(BF16)
        at += w_ref.shape[0]
    for copy in copies:
        copy.wait()


def factors(x_ref, gate_a, gate_b, width, base):
    count = x_ref.shape[0]
    ids = x_ref[:, width:].astype(F32)
    a, b = ids[:, 0:1], ids[:, 1:2]
    logits = gate_a[base : base + count] + gate_b[base : base + count]
    lane = lax.broadcasted_iota(jnp.int32, logits.shape, 1).astype(F32)
    is_a, is_b = lane == a, lane == b
    la = jnp.sum(jnp.where(is_a, logits, 0.0), axis=1, keepdims=True)
    lb = jnp.sum(jnp.where(is_b, logits, 0.0), axis=1, keepdims=True)
    wa = 1.0 / (1.0 + jnp.exp(lb - la))
    wb = 1.0 / (1.0 + jnp.exp(la - lb))
    return jnp.where(is_a, wa, 0.0) + jnp.where(is_b, wb, 0.0)


def hidden_units(e, i, hidden, gate_a, gate_b, up_a, up_b):
    own = slice(e * hidden, (e + 1) * hidden)
    mine = slice(i * hidden, (i + 1) * hidden)
    gate = gate_a[own] + gate_b[own]
    up = up_a[mine] + up_b[mine].astype(F32)
    return (gate / (1.0 + jnp.exp(-gate)) * up).T.astype(BF16)


def hidden_kernel(experts, fetched, gate_a, gate_b, up_a, up_b, down_ref, *refs):
    out_ref, *held, sems = refs
    copies = fetches(down_ref, fetched, held, sems)
    for copy in copies:
        copy.start()
    hidden = out_ref.shape[2]
    for i, e in enumerate(experts):
        out_ref[i] = hidden_units(e, i, hidden, gate_a, gate_b, up_a, up_b)
    for copy in copies:
        copy.wait()


def down_kernel(ready, x_ref, gate_a, gate_b, up_a, up_b, h_ref, down_ref, *refs):
    weights, outs, (held_ref, sems) = refs[:ready], refs[ready : ready + 8], refs[ready + 8 :]
    experts, hidden, width = down_ref.shape
    late = [held_ref.at[i] for i in range(experts - ready)]
    copies = fetches(down_ref, range(ready, experts), late, sems)
    for copy in copies:
        copy.start()
    half = h_ref.shape[0]
    factor = factors(x_ref, gate_a, gate_b, width, experts * hidden)
    total = None
    for e in range(experts):
        if e < half:
            h = h_ref[e]
        else:
            h = hidden_units(e, e - half, hidden, gate_a, gate_b, up_a, up_b)
        if e < ready:
            w = weights[e][...]
        else:
            copies[e - ready].wait()
            w = late[e - ready][...]
        term = factor[:, e : e + 1] * jnp.dot(h, w, preferred_element_type=F32)
        total = term if total is None else total + term
    rows = outs[0].shape[0]
    for j, out in enumerate(outs):
        out[...] = total[j * rows : (j + 1) * rows].astype(out.dtype)


def fast(tokens, expert_ids, router, w_gate, w_up, w_down):
    rows, width = tokens.shape
    experts, hidden, _ = w_gate.shape
    count, half = 8 * rows, experts // 2
    shape = lambda *s, dtype=F32: jax.ShapeDtypeStruct(s, dtype)
    in_hbm = lambda array: pltpu.with_memory_space_constraint(array, pltpu.HBM)
    (own,) = call(
        pack_kernel,
        [shape(rows, width + IDS, dtype=BF16)],
        [in_hbm(tokens), in_hbm(expert_ids.T)],
        30_000_000_000,
        4 * rows * width,
        1,
        [pltpu.VMEM(expert_ids.shape[::-1], jnp.int32), pltpu.SemaphoreType.DMA((2,))],
        hbm=(0, 1),
    )
    far = xor_send(own, 4)
    near = [xor_send(own, k) for k in (1, 2, 3)]
    forwarded = [xor_send(far, k) for k in (1, 2, 3)]
    blocks = [own, *near, far, *forwarded]

    w_gate, w_up, w_down = in_vmem(w_gate), in_hbm(w_up), in_hbm(w_down)
    flops = 2 * count * hidden * width
    size = 2 * hidden * width
    lines = jnp.pad(router.T, ((0, 128 - experts), (0, 0)))
    one = pltpu.VMEM((hidden, width), BF16)
    part_of_one = pltpu.VMEM((hidden // 2, width), BF16)
    sems = lambda n: [pltpu.SemaphoreType.DMA((n,))]
    up0, up1a = call(
        functools.partial(fetch_kernel, (0, (1, 0))),
        [one, part_of_one],
        [far[:, :128], w_up],
        8_000_000_000,
        0,
        1,
        sems(2),
        hbm=(1,),
    )
    x, gate, up1b, up2, up3a = call(
        functools.partial(gate_kernel, ((1, hidden // 2), 2, (3, 0)), 2),
        [
            shape(count, width + IDS, dtype=BF16),
            shape(experts * hidden + count, count),
            part_of_one,
            one,
            part_of_one,
        ],
        [*blocks, lines, w_gate, w_up, up0, up1a],
        experts * flops,
        experts * size,
        3,
        sems(3),
        hbm=(10,),
    )
    gate_other = lax.ppermute(gate, "mp", SWAP)

    def up_call(up_fetched, down_fetched, weights, held, carried):
        n = len(held)
        part, sent, *held = call(
            functools.partial(up_kernel, len(weights), len(carried), up_fetched, down_fetched),
            [
                shape(half * hidden, count),
                shape(half * hidden, count, dtype=BF16),
                *held,
            ],
            [x, w_up, w_down, *weights, *carried],
            half * flops,
            half * size,
            3,
            sems(max(n, 1)),
            hbm=(1, 2),
        )
        return (part, lax.ppermute(sent, "mp", SWAP)), held

    first, (up3b, down0) = up_call(
        ((3, hidden // 2),), (0,), (up0, up1a, up1b), (part_of_one, one), (up3a,)
    )
    second, (down1,) = up_call((), (1,), (up2, up3a, up3b), (one,), ())
    units, down2 = call(
        functools.partial(hidden_kernel, range(half), (2,)),
        [shape(half, count, hidden, dtype=BF16)] + [one] * 1,
        [gate, gate_other, *first, w_down],
        0,
        12 * half * hidden * count,
        4,
        sems(1),
        hbm=(4,),
    )
    parts = call(
        functools.partial(down_kernel, 3),
        [shape(rows, width)] + [shape(rows, width, dtype=BF16)] * 7,
        [x, gate, gate_other, *second, units, w_down, down0, down1, down2],
        experts * flops,
        experts * size,
        10,
        [pltpu.VMEM((1, hidden, width), BF16), *sems(1)],
        hbm=(6,),
    )
    far_sums = [xor_send(parts[4 ^ k], k) for k in (3, 2, 1)]
    near_sums = [xor_send(parts[k], k) for k in (3, 2, 1)]
    add = lambda arrays: sum(a.astype(F32) for a in arrays)
    crossing = xor_send(add([parts[4], *far_sums]).astype(BF16), 4)
    return add([parts[0], *near_sums, crossing]).astype(BF16)


def general(tokens, expert_ids, router, w_gate, w_up, w_down):
    gathered, all_ids = (
        lax.all_gather(tokens, "batch", axis=0, tiled=True),
        lax.all_gather(expert_ids, "batch", axis=0, tiled=True),
    )
    token_count = gathered.shape[0]
    half_width = gathered.shape[1]
    experts = w_gate.shape[0]
    capacity = 3 * token_count // 4
    pair_expert = all_ids.reshape(-1)
    onehot = (pair_expert[:, None] == jnp.arange(experts, dtype=jnp.int32)[None, :]).astype(
        jnp.int32
    )
    position = jnp.sum((jnp.cumsum(onehot, axis=0) - 1) * onehot, axis=1)
    pair_token = jnp.arange(2 * token_count, dtype=jnp.int32) // 2
    slot_token = (
        jnp.full((experts, capacity), token_count, jnp.int32)
        .at[pair_expert, position]
        .set(pair_token)
    )
    slot_rows = jnp.take(gathered, jnp.minimum(slot_token, token_count - 1), axis=0)
    logit_part = jnp.dot(gathered, router, preferred_element_type=F32)
    gate_part = jnp.einsum("ecd,efd->ecf", slot_rows, w_gate, preferred_element_type=F32)
    up_part = jnp.einsum("ecd,efd->ecf", slot_rows, w_up, preferred_element_type=F32)
    logits, gate_sum, up_sum = lax.psum((logit_part, gate_part, up_part), "mp")
    chosen = jnp.take_along_axis(logits, all_ids, axis=1)
    weights = 1.0 / (1.0 + jnp.exp(chosen[:, ::-1] - chosen))
    slot_weight = (
        jnp.zeros((experts, capacity), F32)
        .at[pair_expert, position]
        .set(weights.reshape(-1))
    )
    hidden = (jax.nn.silu(gate_sum) * up_sum).astype(BF16)
    slot_out = (
        jnp.einsum("ecf,efd->ecd", hidden, w_down, preferred_element_type=F32)
        * slot_weight[:, :, None]
    )
    partial_value = (
        jnp.zeros((token_count, half_width), F32)
        .at[slot_token.reshape(-1)]
        .add(slot_out.reshape(-1, half_width), mode="drop")
    )
    mine = lax.psum_scatter(partial_value, "batch", scatter_dimension=0, tiled=True)
    return mine.astype(BF16)


def solution(mesh):
    def per_device(*args):
        rows, (experts, hidden, _) = args[0].shape[0], args[3].shape
        fits = mesh.shape["batch"] == 8 and rows % 16 == 0 and 8 * rows <= 128
        if fits and experts == 4 and hidden <= 1024:
            return fast(*args)
        return general(*args)

    in_specs = (
        P(("group", "batch"), "mp"),
        P(("group", "batch"), None),
        P("mp", None),
        P(None, "batch", "mp"),
        P(None, "batch", "mp"),
        P(None, "batch", "mp"),
    )
    out_specs = P(("group", "batch"), "mp")
    return jax.shard_map(
        per_device, mesh=mesh, in_specs=in_specs, out_specs=out_specs, check_vma=False
    )
```

```python
import functools
import jax
import jax.numpy as jnp
from jax import lax
from jax.experimental import pallas as pl
from jax.experimental.pallas import tpu as pltpu
from jax.sharding import PartitionSpec as P

F32, BF16 = jnp.float32, jnp.bfloat16
IDS = 128
SWAP = [(0, 1), (1, 0)]
HBM_BLOCK = pl.BlockSpec(memory_space=pltpu.HBM)
VMEM_BLOCK = pl.BlockSpec(memory_space=pltpu.VMEM)


def xor_send(block, mask):
    return lax.ppermute(block, "batch", [(i, i ^ mask) for i in range(8)])


def in_vmem(array):
    return pltpu.with_memory_space_constraint(array, pltpu.VMEM)


def call(kernel, outs, args, flops, size, vmem, scratch=(), hbm=()):
    specs = [HBM_BLOCK if i in hbm else VMEM_BLOCK for i in range(len(args))]
    return pl.pallas_call(
        kernel,
        out_shape=outs,
        in_specs=specs,
        out_specs=[VMEM_BLOCK] * len(outs),
        scratch_shapes=list(scratch),
        compiler_params=pltpu.CompilerParams(vmem_limit_bytes=int(vmem * 2**20)),
        cost_estimate=pl.CostEstimate(flops=flops, bytes_accessed=size, transcendentals=0),
    )(*args)


def column(row, rows):
    diagonal = lax.broadcasted_iota(jnp.int32, (rows, rows), 0) == lax.broadcasted_iota(
        jnp.int32, (rows, rows), 1
    )
    return jnp.sum(jnp.where(diagonal, row, 0.0), axis=1, keepdims=True)


def pack_kernel(tokens_ref, ids_ref, out_ref, held_ref, sems):
    rows, width = tokens_ref.shape
    copies = [
        pltpu.make_async_copy(ids_ref, held_ref, sems.at[0]),
        pltpu.make_async_copy(tokens_ref, out_ref.at[:, pl.ds(0, width)], sems.at[1]),
    ]
    for copy in copies:
        copy.start()
    copies[0].wait()
    ids = held_ref[...].astype(F32)
    lane = lax.broadcasted_iota(jnp.int32, (rows, IDS), 1)
    out_ref[:, width:] = jnp.where(
        lane == 0, column(ids[0:1], rows), column(ids[1:2], rows)
    ).astype(BF16)
    copies[1].wait()


def over_width(a, b):
    return lax.dot_general(a, b, (((1,), (1,)), ((), ())), preferred_element_type=F32)


def fetches(source_ref, wanted, targets, sems, at=0):
    copies = []
    for i, (place, target) in enumerate(zip(wanted, targets)):
        rows = target.shape[0]
        e, first = place if isinstance(place, tuple) else (place, 0)
        copies.append(
            pltpu.make_async_copy(
                source_ref.at[e, pl.ds(first, rows)], target, sems.at[at + i]
            )
        )
    return copies


def fetch_kernel(fetched, _, source_ref, *refs):
    *held, sems = refs
    copies = fetches(source_ref, fetched, held, sems)
    for copy in copies:
        copy.start()
    for copy in copies:
        copy.wait()


def gate_kernel(fetched, carried, *refs):
    blocks, (router_ref, w_ref, up_ref), refs = refs[:8], refs[8:11], refs[11 + carried :]
    x_ref, part_ref, *held, sems = refs
    experts, hidden, width = w_ref.shape
    copies = fetches(up_ref, fetched, held, sems)
    for copy in copies:
        copy.start()
    rows = blocks[0].shape[0]
    for j, block in enumerate(blocks):
        x_ref[j * rows : (j + 1) * rows] = block[...]
    x = x_ref[:, :width]
    part_ref[experts * hidden :] = over_width(x, router_ref[...])
    for e in range(experts):
        part_ref[e * hidden : (e + 1) * hidden] = over_width(w_ref[e], x)
    for copy in copies:
        copy.wait()


def up_kernel(ready, carried, up_fetched, down_fetched, x_ref, up_ref, down_ref, *refs):
    weights, (part_ref, sent_ref, *held, sems) = refs[:ready], refs[ready + carried :]
    width = weights[0].shape[1]
    n = len(up_fetched)
    copies = fetches(up_ref, up_fetched, held[:n], sems) + fetches(
        down_ref, down_fetched, held[n:], sems, n
    )
    for copy in copies:
        copy.start()
    x, at = x_ref[:, :width], 0
    for w_ref in weights:
        own = slice(at, at + w_ref.shape[0])
        part = over_width(w_ref[...], x)
        part_ref[own] = part
        sent_ref[own] = part.astype(BF16)
        at += w_ref.shape[0]
    for copy in copies:
        copy.wait()


def factors(x_ref, gate_a, gate_b, width, base):
    count = x_ref.shape[0]
    ids = x_ref[:, width:].astype(F32)
    a, b = ids[:, 0:1], ids[:, 1:2]
    logits = gate_a[base : base + count] + gate_b[base : base + count]
    lane = lax.broadcasted_iota(jnp.int32, logits.shape, 1).astype(F32)
    is_a, is_b = lane == a, lane == b
    la = jnp.sum(jnp.where(is_a, logits, 0.0), axis=1, keepdims=True)
    lb = jnp.sum(jnp.where(is_b, logits, 0.0), axis=1, keepdims=True)
    wa = 1.0 / (1.0 + jnp.exp(lb - la))
    wb = 1.0 / (1.0 + jnp.exp(la - lb))
    return jnp.where(is_a, wa, 0.0) + jnp.where(is_b, wb, 0.0)


def hidden_units(e, i, hidden, gate_a, gate_b, up_a, up_b):
    own = slice(e * hidden, (e + 1) * hidden)
    mine = slice(i * hidden, (i + 1) * hidden)
    gate = gate_a[own] + gate_b[own]
    up = up_a[mine] + up_b[mine].astype(F32)
    return (gate / (1.0 + jnp.exp(-gate)) * up).T.astype(BF16)


def hidden_kernel(experts, fetched, gate_a, gate_b, up_a, up_b, down_ref, *refs):
    out_ref, *held, sems = refs
    copies = fetches(down_ref, fetched, held, sems)
    for copy in copies:
        copy.start()
    hidden = out_ref.shape[2]
    for i, e in enumerate(experts):
        out_ref[i] = hidden_units(e, i, hidden, gate_a, gate_b, up_a, up_b)
    for copy in copies:
        copy.wait()


def down_kernel(ready, x_ref, gate_a, gate_b, up_a, up_b, h_ref, down_ref, *refs):
    weights, outs, (held_ref, sems) = refs[:ready], refs[ready : ready + 8], refs[ready + 8 :]
    experts, hidden, width = down_ref.shape
    late = [held_ref.at[i] for i in range(experts - ready)]
    copies = fetches(down_ref, range(ready, experts), late, sems)
    for copy in copies:
        copy.start()
    half = h_ref.shape[0]
    factor = factors(x_ref, gate_a, gate_b, width, experts * hidden)
    total = None
    for e in range(experts):
        if e < half:
            h = h_ref[e]
        else:
            h = hidden_units(e, e - half, hidden, gate_a, gate_b, up_a, up_b)
        if e < ready:
            w = weights[e][...]
        else:
            copies[e - ready].wait()
            w = late[e - ready][...]
        term = factor[:, e : e + 1] * jnp.dot(h, w, preferred_element_type=F32)
        total = term if total is None else total + term
    rows = outs[0].shape[0]
    for j, out in enumerate(outs):
        out[...] = total[j * rows : (j + 1) * rows].astype(out.dtype)


def fast(tokens, expert_ids, router, w_gate, w_up, w_down):
    rows, width = tokens.shape
    experts, hidden, _ = w_gate.shape
    count, half = 8 * rows, experts // 2
    shape = lambda *s, dtype=F32: jax.ShapeDtypeStruct(s, dtype)
    in_hbm = lambda array: pltpu.with_memory_space_constraint(array, pltpu.HBM)
    (own,) = call(
        pack_kernel,
        [shape(rows, width + IDS, dtype=BF16)],
        [in_hbm(tokens), in_hbm(expert_ids.T)],
        30_000_000_000,
        4 * rows * width,
        1,
        [pltpu.VMEM(expert_ids.shape[::-1], jnp.int32), pltpu.SemaphoreType.DMA((2,))],
        hbm=(0, 1),
    )
    far = xor_send(own, 4)
    near = [xor_send(own, k) for k in (1, 2, 3)]
    forwarded = [xor_send(far, k) for k in (1, 2, 3)]
    blocks = [own, *near, far, *forwarded]

    w_gate, w_up, w_down = in_vmem(w_gate), in_hbm(w_up), in_hbm(w_down)
    flops = 2 * count * hidden * width
    size = 2 * hidden * width
    lines = jnp.pad(router.T, ((0, 128 - experts), (0, 0)))
    one = pltpu.VMEM((hidden, width), BF16)
    part_of_one = pltpu.VMEM((hidden // 2, width), BF16)
    sems = lambda n: [pltpu.SemaphoreType.DMA((n,))]
    tile = hidden // 2
    early = call(
        functools.partial(fetch_kernel, ((0, 0), (0, tile), (1, 0))),
        [part_of_one] * 3,
        [far[:, :128], w_up],
        8_000_000_000,
        0,
        1,
        sems(3),
        hbm=(1,),
    )
    x, gate, *following = call(
        functools.partial(gate_kernel, ((1, tile), (2, 0), (2, tile), (3, 0)), 3),
        [
            shape(count, width + IDS, dtype=BF16),
            shape(experts * hidden + count, count),
            *[part_of_one] * 4,
        ],
        [*blocks, lines, w_gate, w_up, *early],
        experts * flops,
        experts * size,
        3,
        sems(4),
        hbm=(10,),
    )
    gate_other = lax.ppermute(gate, "mp", SWAP)

    def up_call(up_fetched, down_fetched, weights, held, carried):
        n = len(held)
        part, sent, *held = call(
            functools.partial(up_kernel, len(weights), len(carried), up_fetched, down_fetched),
            [
                shape(half * hidden, count),
                shape(half * hidden, count, dtype=BF16),
                *held,
            ],
            [x, w_up, w_down, *weights, *carried],
            half * flops,
            half * size,
            3,
            sems(max(n, 1)),
            hbm=(1, 2),
        )
        return (part, lax.ppermute(sent, "mp", SWAP)), held

    first, (up3b, down0) = up_call(
        ((3, tile),), (0,), (*early, following[0]), (part_of_one, one), ()
    )
    second, (down1,) = up_call((), (1,), (*following[1:], up3b), (one,), ())
    units, down2 = call(
        functools.partial(hidden_kernel, range(half), (2,)),
        [shape(half, count, hidden, dtype=BF16)] + [one] * 1,
        [gate, gate_other, *first, w_down],
        0,
        12 * half * hidden * count,
        4,
        sems(1),
        hbm=(4,),
    )
    parts = call(
        functools.partial(down_kernel, 3),
        [shape(rows, width)] + [shape(rows, width, dtype=BF16)] * 7,
        [x, gate, gate_other, *second, units, w_down, down0, down1, down2],
        experts * flops,
        experts * size,
        10,
        [pltpu.VMEM((1, hidden, width), BF16), *sems(1)],
        hbm=(6,),
    )
    far_sums = [xor_send(parts[4 ^ k], k) for k in (3, 2, 1)]
    near_sums = [xor_send(parts[k], k) for k in (3, 2, 1)]
    add = lambda arrays: sum(a.astype(F32) for a in arrays)
    crossing = xor_send(add([parts[4], *far_sums]).astype(BF16), 4)
    return add([parts[0], *near_sums, crossing]).astype(BF16)


def general(tokens, expert_ids, router, w_gate, w_up, w_down):
    gathered, all_ids = (
        lax.all_gather(tokens, "batch", axis=0, tiled=True),
        lax.all_gather(expert_ids, "batch", axis=0, tiled=True),
    )
    token_count = gathered.shape[0]
    half_width = gathered.shape[1]
    experts = w_gate.shape[0]
    capacity = 3 * token_count // 4
    pair_expert = all_ids.reshape(-1)
    onehot = (pair_expert[:, None] == jnp.arange(experts, dtype=jnp.int32)[None, :]).astype(
        jnp.int32
    )
    position = jnp.sum((jnp.cumsum(onehot, axis=0) - 1) * onehot, axis=1)
    pair_token = jnp.arange(2 * token_count, dtype=jnp.int32) // 2
    slot_token = (
        jnp.full((experts, capacity), token_count, jnp.int32)
        .at[pair_expert, position]
        .set(pair_token)
    )
    slot_rows = jnp.take(gathered, jnp.minimum(slot_token, token_count - 1), axis=0)
    logit_part = jnp.dot(gathered, router, preferred_element_type=F32)
    gate_part = jnp.einsum("ecd,efd->ecf", slot_rows, w_gate, preferred_element_type=F32)
    up_part = jnp.einsum("ecd,efd->ecf", slot_rows, w_up, preferred_element_type=F32)
    logits, gate_sum, up_sum = lax.psum((logit_part, gate_part, up_part), "mp")
    chosen = jnp.take_along_axis(logits, all_ids, axis=1)
    weights = 1.0 / (1.0 + jnp.exp(chosen[:, ::-1] - chosen))
    slot_weight = (
        jnp.zeros((experts, capacity), F32)
        .at[pair_expert, position]
        .set(weights.reshape(-1))
    )
    hidden = (jax.nn.silu(gate_sum) * up_sum).astype(BF16)
    slot_out = (
        jnp.einsum("ecf,efd->ecd", hidden, w_down, preferred_element_type=F32)
        * slot_weight[:, :, None]
    )
    partial_value = (
        jnp.zeros((token_count, half_width), F32)
        .at[slot_token.reshape(-1)]
        .add(slot_out.reshape(-1, half_width), mode="drop")
    )
    mine = lax.psum_scatter(partial_value, "batch", scatter_dimension=0, tiled=True)
    return mine.astype(BF16)


def solution(mesh):
    def per_device(*args):
        rows, (experts, hidden, _) = args[0].shape[0], args[3].shape
        fits = mesh.shape["batch"] == 8 and rows % 16 == 0 and 8 * rows <= 128
        if fits and experts == 4 and hidden <= 1024:
            return fast(*args)
        return general(*args)

    in_specs = (
        P(("group", "batch"), "mp"),
        P(("group", "batch"), None),
        P("mp", None),
        P(None, "batch", "mp"),
        P(None, "batch", "mp"),
        P(None, "batch", "mp"),
    )
    out_specs = P(("group", "batch"), "mp")
    return jax.shard_map(
        per_device, mesh=mesh, in_specs=in_specs, out_specs=out_specs, check_vma=False
    )
```

```python
import functools
import jax
import jax.numpy as jnp
from jax import lax
from jax.experimental import pallas as pl
from jax.experimental.pallas import tpu as pltpu
from jax.sharding import PartitionSpec as P

F32, BF16 = jnp.float32, jnp.bfloat16
IDS = 128
SWAP = [(0, 1), (1, 0)]
HBM_BLOCK = pl.BlockSpec(memory_space=pltpu.HBM)
VMEM_BLOCK = pl.BlockSpec(memory_space=pltpu.VMEM)


def xor_send(block, mask):
    return lax.ppermute(block, "batch", [(i, i ^ mask) for i in range(8)])


def in_vmem(array):
    return pltpu.with_memory_space_constraint(array, pltpu.VMEM)


def call(kernel, outs, args, flops, size, vmem, scratch=(), hbm=()):
    specs = [HBM_BLOCK if i in hbm else VMEM_BLOCK for i in range(len(args))]
    return pl.pallas_call(
        kernel,
        out_shape=outs,
        in_specs=specs,
        out_specs=[VMEM_BLOCK] * len(outs),
        scratch_shapes=list(scratch),
        compiler_params=pltpu.CompilerParams(vmem_limit_bytes=int(vmem * 2**20)),
        cost_estimate=pl.CostEstimate(flops=flops, bytes_accessed=size, transcendentals=0),
    )(*args)


def column(row, rows):
    diagonal = lax.broadcasted_iota(jnp.int32, (rows, rows), 0) == lax.broadcasted_iota(
        jnp.int32, (rows, rows), 1
    )
    return jnp.sum(jnp.where(diagonal, row, 0.0), axis=1, keepdims=True)


def pack_kernel(tokens_ref, ids_ref, out_ref, held_ref, sems):
    rows, width = tokens_ref.shape
    copies = [
        pltpu.make_async_copy(ids_ref, held_ref, sems.at[0]),
        pltpu.make_async_copy(tokens_ref, out_ref.at[:, pl.ds(0, width)], sems.at[1]),
    ]
    for copy in copies:
        copy.start()
    copies[0].wait()
    ids = held_ref[...].astype(F32)
    lane = lax.broadcasted_iota(jnp.int32, (rows, IDS), 1)
    out_ref[:, width:] = jnp.where(
        lane == 0, column(ids[0:1], rows), column(ids[1:2], rows)
    ).astype(BF16)
    copies[1].wait()


def over_width(a, b):
    return lax.dot_general(a, b, (((1,), (1,)), ((), ())), preferred_element_type=F32)


def fetches(source_ref, wanted, targets, sems, at=0):
    copies = []
    for i, (place, target) in enumerate(zip(wanted, targets)):
        rows = target.shape[0]
        e, first = place if isinstance(place, tuple) else (place, 0)
        copies.append(
            pltpu.make_async_copy(
                source_ref.at[e, pl.ds(first, rows)], target, sems.at[at + i]
            )
        )
    return copies


def fetch_kernel(fetched, _, source_ref, *refs):
    *held, sems = refs
    copies = fetches(source_ref, fetched, held, sems)
    for copy in copies:
        copy.start()
    for copy in copies:
        copy.wait()


def gate_kernel(fetched, carried, *refs):
    blocks, (router_ref, w_ref, up_ref), refs = refs[:8], refs[8:11], refs[11 + carried :]
    x_ref, part_ref, *held, sems = refs
    experts, hidden, width = w_ref.shape
    copies = fetches(up_ref, fetched, held, sems)
    for copy in copies:
        copy.start()
    rows = blocks[0].shape[0]
    for j, block in enumerate(blocks):
        x_ref[j * rows : (j + 1) * rows] = block[...]
    x = x_ref[:, :width]
    part_ref[experts * hidden :] = over_width(x, router_ref[...])
    for e in range(experts):
        part_ref[e * hidden : (e + 1) * hidden] = over_width(w_ref[e], x)
    for copy in copies:
        copy.wait()


def up_kernel(ready, carried, up_fetched, down_fetched, x_ref, up_ref, down_ref, *refs):
    weights, (part_ref, sent_ref, *held, sems) = refs[:ready], refs[ready + carried :]
    width = weights[0].shape[1]
    n = len(up_fetched)
    copies = fetches(up_ref, up_fetched, held[:n], sems) + fetches(
        down_ref, down_fetched, held[n:], sems, n
    )
    for copy in copies:
        copy.start()
    x, at = x_ref[:, :width], 0
    for w_ref in weights:
        own = slice(at, at + w_ref.shape[0])
        part = over_width(w_ref[...], x)
        part_ref[own] = part
        sent_ref[own] = part.astype(BF16)
        at += w_ref.shape[0]
    for copy in copies:
        copy.wait()


def factors(x_ref, gate_a, gate_b, width, base):
    count = x_ref.shape[0]
    ids = x_ref[:, width:].astype(F32)
    a, b = ids[:, 0:1], ids[:, 1:2]
    logits = gate_a[base : base + count] + gate_b[base : base + count]
    lane = lax.broadcasted_iota(jnp.int32, logits.shape, 1).astype(F32)
    is_a, is_b = lane == a, lane == b
    la = jnp.sum(jnp.where(is_a, logits, 0.0), axis=1, keepdims=True)
    lb = jnp.sum(jnp.where(is_b, logits, 0.0), axis=1, keepdims=True)
    wa = 1.0 / (1.0 + jnp.exp(lb - la))
    wb = 1.0 / (1.0 + jnp.exp(la - lb))
    return jnp.where(is_a, wa, 0.0) + jnp.where(is_b, wb, 0.0)


def hidden_units(e, i, hidden, gate_a, gate_b, up_a, up_b):
    own = slice(e * hidden, (e + 1) * hidden)
    mine = slice(i * hidden, (i + 1) * hidden)
    gate = gate_a[own] + gate_b[own]
    up = up_a[mine] + up_b[mine].astype(F32)
    return (gate / (1.0 + jnp.exp(-gate)) * up).T.astype(BF16)


def hidden_kernel(experts, fetched, gate_a, gate_b, up_a, up_b, down_ref, *refs):
    out_ref, *held, sems = refs
    copies = fetches(down_ref, fetched, held, sems)
    for copy in copies:
        copy.start()
    hidden = out_ref.shape[2]
    for i, e in enumerate(experts):
        out_ref[i] = hidden_units(e, i, hidden, gate_a, gate_b, up_a, up_b)
    for copy in copies:
        copy.wait()


def down_kernel(ready, x_ref, gate_a, gate_b, up_a, up_b, h_ref, down_ref, *refs):
    weights, outs, (held_ref, sems) = refs[:ready], refs[ready : ready + 8], refs[ready + 8 :]
    experts, hidden, width = down_ref.shape
    late = [held_ref.at[i] for i in range(experts - ready)]
    copies = fetches(down_ref, range(ready, experts), late, sems)
    for copy in copies:
        copy.start()
    half = h_ref.shape[0]
    factor = factors(x_ref, gate_a, gate_b, width, experts * hidden)
    total = None
    for e in range(experts):
        if e < half:
            h = h_ref[e]
        else:
            h = hidden_units(e, e - half, hidden, gate_a, gate_b, up_a, up_b)
        if e < ready:
            w = weights[e][...]
        else:
            copies[e - ready].wait()
            w = late[e - ready][...]
        term = factor[:, e : e + 1] * jnp.dot(h, w, preferred_element_type=F32)
        total = term if total is None else total + term
    rows = outs[0].shape[0]
    for j, out in enumerate(outs):
        out[...] = total[j * rows : (j + 1) * rows].astype(out.dtype)


def fast(tokens, expert_ids, router, w_gate, w_up, w_down):
    rows, width = tokens.shape
    experts, hidden, _ = w_gate.shape
    count, half = 8 * rows, experts // 2
    shape = lambda *s, dtype=F32: jax.ShapeDtypeStruct(s, dtype)
    in_hbm = lambda array: pltpu.with_memory_space_constraint(array, pltpu.HBM)
    (own,) = call(
        pack_kernel,
        [shape(rows, width + IDS, dtype=BF16)],
        [in_hbm(tokens), in_hbm(expert_ids.T)],
        30_000_000_000,
        4 * rows * width,
        1,
        [pltpu.VMEM(expert_ids.shape[::-1], jnp.int32), pltpu.SemaphoreType.DMA((2,))],
        hbm=(0, 1),
    )
    far = xor_send(own, 4)
    near = [xor_send(own, k) for k in (1, 2, 3)]
    forwarded = [xor_send(far, k) for k in (1, 2, 3)]
    blocks = [own, *near, far, *forwarded]

    w_gate, w_up, w_down = in_vmem(w_gate), in_hbm(w_up), in_hbm(w_down)
    flops = 2 * count * hidden * width
    size = 2 * hidden * width
    lines = jnp.pad(router.T, ((0, 128 - experts), (0, 0)))
    one = pltpu.VMEM((hidden, width), BF16)
    part_of_one = pltpu.VMEM((hidden // 2, width), BF16)
    sems = lambda n: [pltpu.SemaphoreType.DMA((n,))]
    tile = hidden // 2
    early = call(
        functools.partial(fetch_kernel, ((0, 0), (0, tile), (1, 0))),
        [part_of_one] * 3,
        [far[:, :128], w_up],
        8_000_000_000,
        0,
        1,
        sems(3),
        hbm=(1,),
    )
    x, gate, *following = call(
        functools.partial(gate_kernel, ((1, tile), (2, 0), (2, tile), (3, 0)), 3),
        [
            shape(count, width + IDS, dtype=BF16),
            shape(experts * hidden + count, count),
            *[part_of_one] * 4,
        ],
        [*blocks, lines, w_gate, w_up, *early],
        experts * flops,
        experts * size,
        3,
        sems(4),
        hbm=(10,),
    )
    gate_other = lax.ppermute(gate, "mp", SWAP)

    def up_call(up_fetched, down_fetched, weights, held, carried):
        n = len(held)
        part, sent, *held = call(
            functools.partial(up_kernel, len(weights), len(carried), up_fetched, down_fetched),
            [
                shape(half * hidden, count),
                shape(half * hidden, count, dtype=BF16),
                *held,
            ],
            [x, w_up, w_down, *weights, *carried],
            half * flops,
            half * size,
            3,
            sems(max(n, 1)),
            hbm=(1, 2),
        )
        return (part, lax.ppermute(sent, "mp", SWAP)), held

    first, (up3b, down0) = up_call(
        ((3, tile),), (0,), (*early, following[0]), (part_of_one, one), ()
    )
    second, (down1,) = up_call((), (1,), (*following[1:], up3b), (one,), ())
    units, down2 = call(
        functools.partial(hidden_kernel, range(half), (2,)),
        [shape(half, count, hidden, dtype=BF16)] + [one] * 1,
        [gate, gate_other, *first, w_down],
        0,
        12 * half * hidden * count,
        4,
        sems(1),
        hbm=(4,),
    )
    parts = call(
        functools.partial(down_kernel, 3),
        [shape(rows, width)] + [shape(rows, width, dtype=BF16)] * 7,
        [x, gate, gate_other, *second, units, w_down, down0, down1, down2],
        experts * flops,
        experts * size,
        10,
        [pltpu.VMEM((1, hidden, width), BF16), *sems(1)],
        hbm=(6,),
    )
    far_sums = [xor_send(parts[4 ^ k], k) for k in (3, 2, 1)]
    near_sums = [xor_send(parts[k], k) for k in (2, 1, 3)]
    add = lambda arrays: sum(a.astype(F32) for a in arrays)
    crossing = xor_send(add([parts[4], *far_sums]).astype(BF16), 4)
    return add([parts[0], *near_sums, crossing]).astype(BF16)


def general(tokens, expert_ids, router, w_gate, w_up, w_down):
    gathered, all_ids = (
        lax.all_gather(tokens, "batch", axis=0, tiled=True),
        lax.all_gather(expert_ids, "batch", axis=0, tiled=True),
    )
    token_count = gathered.shape[0]
    half_width = gathered.shape[1]
    experts = w_gate.shape[0]
    capacity = 3 * token_count // 4
    pair_expert = all_ids.reshape(-1)
    onehot = (pair_expert[:, None] == jnp.arange(experts, dtype=jnp.int32)[None, :]).astype(
        jnp.int32
    )
    position = jnp.sum((jnp.cumsum(onehot, axis=0) - 1) * onehot, axis=1)
    pair_token = jnp.arange(2 * token_count, dtype=jnp.int32) // 2
    slot_token = (
        jnp.full((experts, capacity), token_count, jnp.int32)
        .at[pair_expert, position]
        .set(pair_token)
    )
    slot_rows = jnp.take(gathered, jnp.minimum(slot_token, token_count - 1), axis=0)
    logit_part = jnp.dot(gathered, router, preferred_element_type=F32)
    gate_part = jnp.einsum("ecd,efd->ecf", slot_rows, w_gate, preferred_element_type=F32)
    up_part = jnp.einsum("ecd,efd->ecf", slot_rows, w_up, preferred_element_type=F32)
    logits, gate_sum, up_sum = lax.psum((logit_part, gate_part, up_part), "mp")
    chosen = jnp.take_along_axis(logits, all_ids, axis=1)
    weights = 1.0 / (1.0 + jnp.exp(chosen[:, ::-1] - chosen))
    slot_weight = (
        jnp.zeros((experts, capacity), F32)
        .at[pair_expert, position]
        .set(weights.reshape(-1))
    )
    hidden = (jax.nn.silu(gate_sum) * up_sum).astype(BF16)
    slot_out = (
        jnp.einsum("ecf,efd->ecd", hidden, w_down, preferred_element_type=F32)
        * slot_weight[:, :, None]
    )
    partial_value = (
        jnp.zeros((token_count, half_width), F32)
        .at[slot_token.reshape(-1)]
        .add(slot_out.reshape(-1, half_width), mode="drop")
    )
    mine = lax.psum_scatter(partial_value, "batch", scatter_dimension=0, tiled=True)
    return mine.astype(BF16)


def solution(mesh):
    def per_device(*args):
        rows, (experts, hidden, _) = args[0].shape[0], args[3].shape
        fits = mesh.shape["batch"] == 8 and rows % 16 == 0 and 8 * rows <= 128
        if fits and experts == 4 and hidden <= 1024:
            return fast(*args)
        return general(*args)

    in_specs = (
        P(("group", "batch"), "mp"),
        P(("group", "batch"), None),
        P("mp", None),
        P(None, "batch", "mp"),
        P(None, "batch", "mp"),
        P(None, "batch", "mp"),
    )
    out_specs = P(("group", "batch"), "mp")
    return jax.shard_map(
        per_device, mesh=mesh, in_specs=in_specs, out_specs=out_specs, check_vma=False
    )
```

```python
import functools
import jax
import jax.numpy as jnp
from jax import lax
from jax.experimental import pallas as pl
from jax.experimental.pallas import tpu as pltpu
from jax.sharding import PartitionSpec as P

F32, BF16 = jnp.float32, jnp.bfloat16
IDS = 128
SWAP = [(0, 1), (1, 0)]
HBM_BLOCK = pl.BlockSpec(memory_space=pltpu.HBM)
VMEM_BLOCK = pl.BlockSpec(memory_space=pltpu.VMEM)


def xor_send(block, mask):
    return lax.ppermute(block, "batch", [(i, i ^ mask) for i in range(8)])


def in_vmem(array):
    return pltpu.with_memory_space_constraint(array, pltpu.VMEM)


def call(kernel, outs, args, flops, size, vmem, scratch=(), hbm=()):
    specs = [HBM_BLOCK if i in hbm else VMEM_BLOCK for i in range(len(args))]
    return pl.pallas_call(
        kernel,
        out_shape=outs,
        in_specs=specs,
        out_specs=[VMEM_BLOCK] * len(outs),
        scratch_shapes=list(scratch),
        compiler_params=pltpu.CompilerParams(vmem_limit_bytes=int(vmem * 2**20)),
        cost_estimate=pl.CostEstimate(flops=flops, bytes_accessed=size, transcendentals=0),
    )(*args)


def column(row, rows):
    diagonal = lax.broadcasted_iota(jnp.int32, (rows, rows), 0) == lax.broadcasted_iota(
        jnp.int32, (rows, rows), 1
    )
    return jnp.sum(jnp.where(diagonal, row, 0.0), axis=1, keepdims=True)


def pack_kernel(tokens_ref, ids_ref, out_ref, held_ref, sems):
    rows, width = tokens_ref.shape
    copies = [
        pltpu.make_async_copy(ids_ref, held_ref, sems.at[0]),
        pltpu.make_async_copy(tokens_ref, out_ref.at[:, pl.ds(0, width)], sems.at[1]),
    ]
    for copy in copies:
        copy.start()
    copies[0].wait()
    ids = held_ref[...].astype(F32)
    lane = lax.broadcasted_iota(jnp.int32, (rows, IDS), 1)
    out_ref[:, width:] = jnp.where(
        lane == 0, column(ids[0:1], rows), column(ids[1:2], rows)
    ).astype(BF16)
    copies[1].wait()


def over_width(a, b):
    return lax.dot_general(a, b, (((1,), (1,)), ((), ())), preferred_element_type=F32)


def fetches(source_ref, wanted, targets, sems, at=0):
    copies = []
    for i, (place, target) in enumerate(zip(wanted, targets)):
        rows = target.shape[0]
        e, first = place if isinstance(place, tuple) else (place, 0)
        copies.append(
            pltpu.make_async_copy(
                source_ref.at[e, pl.ds(first, rows)], target, sems.at[at + i]
            )
        )
    return copies


def fetch_kernel(fetched, _, source_ref, *refs):
    *held, sems = refs
    copies = fetches(source_ref, fetched, held, sems)
    for copy in copies:
        copy.start()
    for copy in copies:
        copy.wait()


def gate_kernel(fetched, carried, *refs):
    blocks, (router_ref, w_ref, up_ref), refs = refs[:8], refs[8:11], refs[11 + carried :]
    x_ref, part_ref, *held, sems = refs
    experts, hidden, width = w_ref.shape
    copies = fetches(up_ref, fetched, held, sems)
    for copy in copies:
        copy.start()
    rows = blocks[0].shape[0]
    for j, block in enumerate(blocks):
        x_ref[j * rows : (j + 1) * rows] = block[...]
    x = x_ref[:, :width]
    part_ref[experts * hidden :] = over_width(x, router_ref[...])
    for e in range(experts):
        part_ref[e * hidden : (e + 1) * hidden] = over_width(w_ref[e], x)
    for copy in copies:
        copy.wait()


def up_kernel(ready, carried, up_fetched, down_fetched, x_ref, up_ref, down_ref, *refs):
    weights, (part_ref, sent_ref, *held, sems) = refs[:ready], refs[ready + carried :]
    width = weights[0].shape[1]
    n = len(up_fetched)
    copies = fetches(up_ref, up_fetched, held[:n], sems) + fetches(
        down_ref, down_fetched, held[n:], sems, n
    )
    for copy in copies:
        copy.start()
    x, at = x_ref[:, :width], 0
    for w_ref in weights:
        own = slice(at, at + w_ref.shape[0])
        part = over_width(w_ref[...], x)
        part_ref[own] = part
        sent_ref[own] = part.astype(BF16)
        at += w_ref.shape[0]
    for copy in copies:
        copy.wait()


def factors(x_ref, gate_a, gate_b, width, base):
    count = x_ref.shape[0]
    ids = x_ref[:, width:].astype(F32)
    a, b = ids[:, 0:1], ids[:, 1:2]
    logits = gate_a[base : base + count] + gate_b[base : base + count]
    lane = lax.broadcasted_iota(jnp.int32, logits.shape, 1).astype(F32)
    is_a, is_b = lane == a, lane == b
    la = jnp.sum(jnp.where(is_a, logits, 0.0), axis=1, keepdims=True)
    lb = jnp.sum(jnp.where(is_b, logits, 0.0), axis=1, keepdims=True)
    wa = 1.0 / (1.0 + jnp.exp(lb - la))
    wb = 1.0 / (1.0 + jnp.exp(la - lb))
    return jnp.where(is_a, wa, 0.0) + jnp.where(is_b, wb, 0.0)


def hidden_units(e, i, hidden, gate_a, gate_b, up_a, up_b):
    own = slice(e * hidden, (e + 1) * hidden)
    mine = slice(i * hidden, (i + 1) * hidden)
    gate = gate_a[own] + gate_b[own]
    up = up_a[mine] + up_b[mine].astype(F32)
    return (gate / (1.0 + jnp.exp(-gate)) * up).T.astype(BF16)


def hidden_kernel(experts, fetched, gate_a, gate_b, up_a, up_b, down_ref, *refs):
    out_ref, *held, sems = refs
    copies = fetches(down_ref, fetched, held, sems)
    for copy in copies:
        copy.start()
    hidden = out_ref.shape[2]
    for i, e in enumerate(experts):
        out_ref[i] = hidden_units(e, i, hidden, gate_a, gate_b, up_a, up_b)
    for copy in copies:
        copy.wait()


def down_kernel(ready, x_ref, gate_a, gate_b, up_a, up_b, h_ref, down_ref, *refs):
    weights, outs, (held_ref, sems) = refs[:ready], refs[ready : ready + 8], refs[ready + 8 :]
    experts, hidden, width = down_ref.shape
    late = [held_ref.at[i] for i in range(experts - ready)]
    copies = fetches(down_ref, range(ready, experts), late, sems)
    for copy in copies:
        copy.start()
    half = h_ref.shape[0]
    factor = factors(x_ref, gate_a, gate_b, width, experts * hidden)
    total = None
    for e in range(experts):
        if e < half:
            h = h_ref[e]
        else:
            h = hidden_units(e, e - half, hidden, gate_a, gate_b, up_a, up_b)
        if e < ready:
            w = weights[e][...]
        else:
            copies[e - ready].wait()
            w = late[e - ready][...]
        term = factor[:, e : e + 1] * jnp.dot(h, w, preferred_element_type=F32)
        total = term if total is None else total + term
    rows = outs[0].shape[0]
    for j, out in enumerate(outs):
        out[...] = total[j * rows : (j + 1) * rows].astype(out.dtype)


def fast(tokens, expert_ids, router, w_gate, w_up, w_down):
    rows, width = tokens.shape
    experts, hidden, _ = w_gate.shape
    count, half = 8 * rows, experts // 2
    shape = lambda *s, dtype=F32: jax.ShapeDtypeStruct(s, dtype)
    in_hbm = lambda array: pltpu.with_memory_space_constraint(array, pltpu.HBM)
    (own,) = call(
        pack_kernel,
        [shape(rows, width + IDS, dtype=BF16)],
        [in_hbm(tokens), in_hbm(expert_ids.T)],
        30_000_000_000,
        4 * rows * width,
        1,
        [pltpu.VMEM(expert_ids.shape[::-1], jnp.int32), pltpu.SemaphoreType.DMA((2,))],
        hbm=(0, 1),
    )
    far = xor_send(own, 4)
    near = [xor_send(own, k) for k in (1, 2, 3)]
    forwarded = [xor_send(far, k) for k in (1, 2, 3)]
    blocks = [own, *near, far, *forwarded]

    w_gate, w_up, w_down = in_vmem(w_gate), in_hbm(w_up), in_hbm(w_down)
    flops = 2 * count * hidden * width
    size = 2 * hidden * width
    lines = jnp.pad(router.T, ((0, 128 - experts), (0, 0)))
    one = pltpu.VMEM((hidden, width), BF16)
    part_of_one = pltpu.VMEM((hidden // 2, width), BF16)
    sems = lambda n: [pltpu.SemaphoreType.DMA((n,))]
    tile = hidden // 2
    early = call(
        functools.partial(fetch_kernel, ((0, 0), (0, tile), (1, 0))),
        [part_of_one] * 3,
        [far[:, :128], w_up],
        8_000_000_000,
        0,
        1,
        sems(3),
        hbm=(1,),
    )
    x, gate, *following = call(
        functools.partial(gate_kernel, ((1, tile), (2, 0), (2, tile), (3, 0)), 3),
        [
            shape(count, width + IDS, dtype=BF16),
            shape(experts * hidden + count, count),
            *[part_of_one] * 4,
        ],
        [*blocks, lines, w_gate, w_up, *early],
        experts * flops,
        experts * size,
        3,
        sems(4),
        hbm=(10,),
    )
    gate_other = lax.ppermute(gate, "mp", SWAP)

    def up_call(up_fetched, down_fetched, weights, held, carried):
        n = len(held)
        part, sent, *held = call(
            functools.partial(up_kernel, len(weights), len(carried), up_fetched, down_fetched),
            [
                shape(half * hidden, count),
                shape(half * hidden, count, dtype=BF16),
                *held,
            ],
            [x, w_up, w_down, *weights, *carried],
            half * flops,
            half * size,
            3,
            sems(max(n, 1)),
            hbm=(1, 2),
        )
        return (part, lax.ppermute(sent, "mp", SWAP)), held

    first, (up3b, down0) = up_call(
        ((3, tile),), (0,), (*early, following[0]), (part_of_one, one), ()
    )
    second, (down1,) = up_call((), (1,), (*following[1:], up3b), (one,), ())
    units, down2 = call(
        functools.partial(hidden_kernel, range(half), (2,)),
        [shape(half, count, hidden, dtype=BF16)] + [one] * 1,
        [gate, gate_other, *first, w_down],
        0,
        12 * half * hidden * count,
        4,
        sems(1),
        hbm=(4,),
    )
    parts = call(
        functools.partial(down_kernel, 3),
        [shape(rows, width)] + [shape(rows, width, dtype=BF16)] * 7,
        [x, gate, gate_other, *second, units, w_down, down0, down1, down2],
        experts * flops,
        experts * size,
        10,
        [pltpu.VMEM((1, hidden, width), BF16), *sems(1)],
        hbm=(6,),
    )
    far_sums = [xor_send(parts[4 ^ k], k) for k in (3, 1, 2)]
    near_sums = [xor_send(parts[k], k) for k in (1, 2, 3)]
    add = lambda arrays: sum(a.astype(F32) for a in arrays)
    crossing = xor_send(add([parts[4], *far_sums]).astype(BF16), 4)
    return add([parts[0], *near_sums, crossing]).astype(BF16)


def general(tokens, expert_ids, router, w_gate, w_up, w_down):
    gathered, all_ids = (
        lax.all_gather(tokens, "batch", axis=0, tiled=True),
        lax.all_gather(expert_ids, "batch", axis=0, tiled=True),
    )
    token_count = gathered.shape[0]
    half_width = gathered.shape[1]
    experts = w_gate.shape[0]
    capacity = 3 * token_count // 4
    pair_expert = all_ids.reshape(-1)
    onehot = (pair_expert[:, None] == jnp.arange(experts, dtype=jnp.int32)[None, :]).astype(
        jnp.int32
    )
    position = jnp.sum((jnp.cumsum(onehot, axis=0) - 1) * onehot, axis=1)
    pair_token = jnp.arange(2 * token_count, dtype=jnp.int32) // 2
    slot_token = (
        jnp.full((experts, capacity), token_count, jnp.int32)
        .at[pair_expert, position]
        .set(pair_token)
    )
    slot_rows = jnp.take(gathered, jnp.minimum(slot_token, token_count - 1), axis=0)
    logit_part = jnp.dot(gathered, router, preferred_element_type=F32)
    gate_part = jnp.einsum("ecd,efd->ecf", slot_rows, w_gate, preferred_element_type=F32)
    up_part = jnp.einsum("ecd,efd->ecf", slot_rows, w_up, preferred_element_type=F32)
    logits, gate_sum, up_sum = lax.psum((logit_part, gate_part, up_part), "mp")
    chosen = jnp.take_along_axis(logits, all_ids, axis=1)
    weights = 1.0 / (1.0 + jnp.exp(chosen[:, ::-1] - chosen))
    slot_weight = (
        jnp.zeros((experts, capacity), F32)
        .at[pair_expert, position]
        .set(weights.reshape(-1))
    )
    hidden = (jax.nn.silu(gate_sum) * up_sum).astype(BF16)
    slot_out = (
        jnp.einsum("ecf,efd->ecd", hidden, w_down, preferred_element_type=F32)
        * slot_weight[:, :, None]
    )
    partial_value = (
        jnp.zeros((token_count, half_width), F32)
        .at[slot_token.reshape(-1)]
        .add(slot_out.reshape(-1, half_width), mode="drop")
    )
    mine = lax.psum_scatter(partial_value, "batch", scatter_dimension=0, tiled=True)
    return mine.astype(BF16)


def solution(mesh):
    def per_device(*args):
        rows, (experts, hidden, _) = args[0].shape[0], args[3].shape
        fits = mesh.shape["batch"] == 8 and rows % 16 == 0 and 8 * rows <= 128
        if fits and experts == 4 and hidden <= 1024:
            return fast(*args)
        return general(*args)

    in_specs = (
        P(("group", "batch"), "mp"),
        P(("group", "batch"), None),
        P("mp", None),
        P(None, "batch", "mp"),
        P(None, "batch", "mp"),
        P(None, "batch", "mp"),
    )
    out_specs = P(("group", "batch"), "mp")
    return jax.shard_map(
        per_device, mesh=mesh, in_specs=in_specs, out_specs=out_specs, check_vma=False
    )
```
